128 devices in a mesh: gx: 32 (over x, y, z_hi), gy: 2 (over z_lo), gz: 2 (over core).
Axes of the slice: x: 4, y: 4, z: 4 (z_hi: 2, z_lo: 2; z = z_hi * 2 + z_lo), core: 2. Of those that a mesh axis runs over, the one named last changes fastest.
Arguments:
- initial: float32 [128, 256, 256], P('gx', 'gy', 'gz'), may hold values from -6 to 6
- material: int32 [128, 256, 256], P('gx', 'gy', 'gz'), may hold values from 0 to 7
- conduct: float32 [8], replicated, may hold values from 0.25 to 2
- capacity: float32 [8], replicated, may hold values from 1 to 4
- substeps: int32 [32, 2, 2], P('gx', 'gy', 'gz'), may hold values from 1 to 2
- trace_x: float32 [64, 2, 256, 256], P('gx', None, 'gy', 'gz'), may hold values from -12 to 12
- trace_y: float32 [2, 128, 4, 256], P(None, 'gx', 'gy', 'gz'), may hold values from -12 to 12
- trace_z: float32 [2, 4, 128, 256], P(None, 'gz', 'gx', 'gy'), may hold values from -12 to 12
Outputs:
- thermal_level_field: float32 [128, 256, 256], P('gx', 'gy', 'gz')
- converged_mixed_first: float32 [64, 2, 256, 256], P('gx', None, 'gy', 'gz')
- converged_mixed_second: float32 [2, 128, 4, 256], P(None, 'gx', 'gy', 'gz')
- converged_mixed_third: float32 [2, 4, 128, 256], P(None, 'gz', 'gx', 'gy')
The draws below stay inside these ranges and needn't reach their ends.
Inputs may be any that keep to these rules, and one draw needn't show every extreme that they name: Each subdomain takes 1 or 2 substeps per coarse step.
All inputs are finite; a program needn't handle non-finite values.
Results may differ from the reference program's by a relative error of at most 0.0003.
Values sent between devices are 32-bit elements; how exact they have to be, the bound alone decides.
No kernel may reach another device: no remote copies, remote signals or barrier semaphores. Data moves between devices by JAX's collectives and lax.ppermute only.
A program may use at most 128 MiB of HBM per device.

```python
import math
import jax
import jax.numpy as jnp
from jax import lax

PIECE_SPAN_FIRST = 4
PIECE_SPAN_SECOND = 128
PIECE_SPAN_THIRD = 128
NT = 2
SWEEPS = 8
ITERS = 4
NMAT = 8
MESH_SPAN_FIRST = 128
MESH_SPAN_SECOND = 256
MESH_SPAN_THIRD = 256
N_GX = 32
N_GY = 2
N_GZ = 2


def place_ends(values, key, smallest, largest):
    spot = [jax.random.randint(jax.random.fold_in(key, axis), (), 0, length) for axis, length in enumerate(values.shape)]
    main_axis = values.shape.index(max(values.shape))
    beside = spot[:main_axis] + [(spot[main_axis] + 1) % values.shape[main_axis]] + spot[main_axis + 1:]
    return values.at[tuple(spot)].set(smallest).at[tuple(beside)].set(largest)


def block_scale(stream_key, shape, cuts, low, largest):
    gain = 1.0
    for axis_at, parts in cuts:
        draws = jax.random.uniform(jax.random.fold_in(jax.random.fold_in(stream_key, 6), axis_at), (parts,), jnp.float32, low / len(cuts), largest / len(cuts))
        gain = gain * jnp.repeat(jnp.exp(draws), shape[axis_at] // parts).reshape((-1,) + (1,) * (len(shape) - 1 - axis_at))
    return gain


def gaussian(stream_key, shape, spread, limit, shards=(), dtype=jnp.bfloat16):
    entries = spread * jax.random.normal(stream_key, shape, jnp.float32)
    if shards:
        entries = entries * block_scale(stream_key, shape, shards, -0.22, 0.18)
    return jnp.clip(entries, -limit, limit).astype(dtype)


def setup_inputs(seed: int = 0) -> dict:
    seeds = jax.random.split(jax.random.key(seed), 9)
    return {
        "initial": gaussian(seeds[0], (MESH_SPAN_FIRST, MESH_SPAN_SECOND, MESH_SPAN_THIRD), 1.0, 6.0, ((0, 32), (1, 2), (2, 2)), jnp.float32),
        "material": place_ends(jax.random.randint(seeds[1], (MESH_SPAN_FIRST, MESH_SPAN_SECOND, MESH_SPAN_THIRD), 0, NMAT), jax.random.fold_in(seeds[1], 1), 0, NMAT - 1).astype(jnp.int32),
        "conduct": jnp.clip(jnp.exp(jax.random.uniform(seeds[2], (NMAT,), jnp.float32, math.log(0.25), math.log(2.0))), 0.25, 2.0),
        "capacity": jnp.clip(jnp.exp(jax.random.uniform(seeds[3], (NMAT,), jnp.float32, math.log(1.0), math.log(4.0))), 1.0, 4.0),
        "substeps": place_ends(jax.random.randint(seeds[4], (N_GX, N_GY, N_GZ), 1, 3), jax.random.fold_in(seeds[4], 1), 1, 2).astype(jnp.int32),
        "trace_x": gaussian(seeds[5], (2 * N_GX, NT, MESH_SPAN_SECOND, MESH_SPAN_THIRD), 2.0, 12.0, ((0, 32), (2, 2), (3, 2)), jnp.float32),
        "trace_y": gaussian(seeds[6], (NT, MESH_SPAN_FIRST, 2 * N_GY, MESH_SPAN_THIRD), 2.0, 12.0, ((1, 32), (2, 2), (3, 2)), jnp.float32),
        "trace_z": gaussian(seeds[7], (NT, 2 * N_GZ, MESH_SPAN_FIRST, MESH_SPAN_SECOND), 2.0, 12.0, ((1, 2), (2, 32), (3, 2)), jnp.float32),
    }


p_robin = 1.5
dt_coarse = 0.5
rho_bound = 0.9


def lookup(material, table):
    summed = jnp.zeros(material.shape, jnp.float32)
    for number in range(table.shape[0]):
        summed = summed + jnp.where(material == number, table[number], jnp.float32(0.0))
    return summed


def harmonic(left_k, right_k):
    return 2.0 * left_k * right_k / (left_k + right_k)


def couplings(kcell):
    zero_x = jnp.zeros((1,) + kcell.shape[1:], jnp.float32)
    cond_x = jnp.concatenate([zero_x, harmonic(kcell[:-1], kcell[1:]), zero_x], 0)
    zero_y = jnp.zeros((kcell.shape[0], 1, kcell.shape[2]), jnp.float32)
    cond_y = jnp.concatenate([zero_y, harmonic(kcell[:, :-1], kcell[:, 1:]), zero_y], 1)
    zero_z = jnp.zeros(kcell.shape[:2] + (1,), jnp.float32)
    cond_z = jnp.concatenate([zero_z, harmonic(kcell[:, :, :-1], kcell[:, :, 1:]), zero_z], 2)
    return cond_x, cond_y, cond_z


def boundary_count(extent):
    counted = jnp.zeros(extent, jnp.float32)
    for direction in range(3):
        position = lax.broadcasted_iota(jnp.int32, extent, direction)
        counted = counted + (position == 0).astype(jnp.float32) + (position == extent[direction] - 1).astype(jnp.float32)
    return counted


def neighbours(field, cond_x, cond_y, cond_z):
    padded = jnp.pad(field, ((1, 1), (0, 0), (0, 0)))
    summed = cond_x[1:] * padded[2:] + cond_x[:-1] * padded[:-2]
    padded = jnp.pad(field, ((0, 0), (1, 1), (0, 0)))
    summed = summed + cond_y[:, 1:] * padded[:, 2:] + cond_y[:, :-1] * padded[:, :-2]
    padded = jnp.pad(field, ((0, 0), (0, 0), (1, 1)))
    summed = summed + cond_z[:, :, 1:] * padded[:, :, 2:] + cond_z[:, :, :-1] * padded[:, :, :-2]
    return summed


def prepare(material, conduct, capacity):
    kcell = lookup(material, conduct)
    heat_cap = lookup(material, capacity)
    cond_x, cond_y, cond_z = couplings(kcell)
    base_diag = cond_x[1:] + cond_x[:-1] + cond_y[:, 1:] + cond_y[:, :-1] + cond_z[:, :, 1:] + cond_z[:, :, :-1]
    base_diag = base_diag + p_robin * boundary_count(material.shape)
    return heat_cap, base_diag, cond_x, cond_y, cond_z


def robin_load(extent, face_x, face_y, face_z):
    loaded = jnp.zeros(extent, jnp.float32)
    loaded = loaded.at[0].add(face_x[0]).at[-1].add(face_x[1])
    loaded = loaded.at[:, 0].add(face_y[:, 0]).at[:, -1].add(face_y[:, 1])
    loaded = loaded.at[:, :, 0].add(face_z[0]).at[:, :, -1].add(face_z[1])
    return loaded


def faces(field):
    face_x = jnp.stack([field[0], field[-1]], 0)
    face_y = jnp.stack([field[:, 0], field[:, -1]], 1)
    face_z = jnp.stack([field[:, :, 0], field[:, :, -1]], 0)
    return face_x, face_y, face_z


def substep(field, inertia, prepared, loaded):
    heat_cap, base_diag, cond_x, cond_y, cond_z = prepared
    diagonal = inertia + base_diag
    rhs_side = inertia * field + loaded
    current = field
    for sweep_index in range(SWEEPS):
        weight_m = 1.0 / (1.0 + rho_bound * math.cos(math.pi * (2 * sweep_index + 1) / (2 * SWEEPS)))
        residual = rhs_side - diagonal * current + neighbours(current, cond_x, cond_y, cond_z)
        current = current + weight_m * residual / diagonal
    return current


def advance(field, flag, prepared, in_x, in_y, in_z):
    heat_cap = prepared[0]
    loaded = robin_load(field.shape, in_x, in_y, in_z)

    def slow_path(state):
        updated = substep(state, heat_cap / dt_coarse, prepared, loaded)
        return (updated,) + faces(updated)

    def fast_path(state):
        midway = substep(state, 2.0 * heat_cap / dt_coarse, prepared, loaded)
        updated = substep(midway, 2.0 * heat_cap / dt_coarse, prepared, loaded)
        first = faces(midway)
        second = faces(updated)
        return (updated, 0.5 * (first[0] + second[0]), 0.5 * (first[1] + second[1]), 0.5 * (first[2] + second[2]))

    return lax.cond(flag == 2, fast_path, slow_path, field)


def window(initial, material, flag, in_x, in_y, in_z, conduct, capacity):
    prepared = prepare(material, conduct, capacity)
    field = initial
    sent_x, sent_y, sent_z = [], [], []
    for moment in range(NT):
        field, mean_x, mean_y, mean_z = advance(field, flag, prepared, in_x[:, moment], in_y[moment], in_z[moment])
        sent_x.append(2.0 * p_robin * mean_x - in_x[:, moment])
        sent_y.append(2.0 * p_robin * mean_y - in_y[moment])
        sent_z.append(2.0 * p_robin * mean_z - in_z[moment])
    return field, jnp.stack(sent_x, 1), jnp.stack(sent_y, 0), jnp.stack(sent_z, 0)


def reference(initial, material, conduct, capacity, substeps, trace_x, trace_y, trace_z):
    block_count = N_GX * N_GY * N_GZ

    def split(whole):
        return whole.reshape(N_GX, PIECE_SPAN_FIRST, N_GY, PIECE_SPAN_SECOND, N_GZ, PIECE_SPAN_THIRD).transpose(0, 2, 4, 1, 3, 5).reshape(block_count, PIECE_SPAN_FIRST, PIECE_SPAN_SECOND, PIECE_SPAN_THIRD)

    blocks_field = split(initial)
    blocks_mat = split(material)
    flag_list = substeps.reshape(block_count)
    got_x = trace_x.reshape(N_GX, 2, NT, N_GY, PIECE_SPAN_SECOND, N_GZ, PIECE_SPAN_THIRD).transpose(0, 3, 5, 1, 2, 4, 6)
    got_y = trace_y.reshape(NT, N_GX, PIECE_SPAN_FIRST, N_GY, 2, N_GZ, PIECE_SPAN_THIRD).transpose(1, 3, 5, 0, 2, 4, 6)
    got_z = trace_z.reshape(NT, N_GZ, 2, N_GX, PIECE_SPAN_FIRST, N_GY, PIECE_SPAN_SECOND).transpose(3, 5, 1, 0, 2, 4, 6)
    computed_answer = blocks_field
    for iteration in range(ITERS):
        def solve_block(bundle):
            return window(*bundle, conduct, capacity)

        computed_answer, out_x, out_y, out_z = lax.map(solve_block, (blocks_field, blocks_mat, flag_list,
                                                            got_x.reshape(block_count, 2, NT, PIECE_SPAN_SECOND, PIECE_SPAN_THIRD),
                                                            got_y.reshape(block_count, NT, PIECE_SPAN_FIRST, 2, PIECE_SPAN_THIRD),
                                                            got_z.reshape(block_count, NT, 2, PIECE_SPAN_FIRST, PIECE_SPAN_SECOND)))
        out_x = out_x.reshape(N_GX, N_GY, N_GZ, 2, NT, PIECE_SPAN_SECOND, PIECE_SPAN_THIRD)
        out_y = out_y.reshape(N_GX, N_GY, N_GZ, NT, PIECE_SPAN_FIRST, 2, PIECE_SPAN_THIRD)
        out_z = out_z.reshape(N_GX, N_GY, N_GZ, NT, 2, PIECE_SPAN_FIRST, PIECE_SPAN_SECOND)
        low_side = jnp.concatenate([got_x[:1, :, :, 0], out_x[:-1, :, :, 1]], 0)
        high_side = jnp.concatenate([out_x[1:, :, :, 0], got_x[-1:, :, :, 1]], 0)
        got_x = jnp.stack([low_side, high_side], 3)
        low_side = jnp.concatenate([got_y[:, :1, :, :, :, 0], out_y[:, :-1, :, :, :, 1]], 1)
        high_side = jnp.concatenate([out_y[:, 1:, :, :, :, 0], got_y[:, -1:, :, :, :, 1]], 1)
        got_y = jnp.stack([low_side, high_side], 5)
        low_side = jnp.concatenate([got_z[:, :, :1, :, 0], out_z[:, :, :-1, :, 1]], 2)
        high_side = jnp.concatenate([out_z[:, :, 1:, :, 0], got_z[:, :, -1:, :, 1]], 2)
        got_z = jnp.stack([low_side, high_side], 4)
    thermal_level_field = computed_answer.reshape(N_GX, N_GY, N_GZ, PIECE_SPAN_FIRST, PIECE_SPAN_SECOND, PIECE_SPAN_THIRD).transpose(0, 3, 1, 4, 2, 5).reshape(MESH_SPAN_FIRST, MESH_SPAN_SECOND, MESH_SPAN_THIRD)
    converged_mixed_first = got_x.transpose(0, 3, 4, 1, 5, 2, 6).reshape(2 * N_GX, NT, MESH_SPAN_SECOND, MESH_SPAN_THIRD)
    converged_mixed_second = got_y.transpose(3, 0, 4, 1, 5, 2, 6).reshape(NT, MESH_SPAN_FIRST, 2 * N_GY, MESH_SPAN_THIRD)
    converged_mixed_third = got_z.transpose(3, 2, 4, 0, 5, 1, 6).reshape(NT, 2 * N_GZ, MESH_SPAN_FIRST, MESH_SPAN_SECOND)
    return thermal_level_field, converged_mixed_first, converged_mixed_second, converged_mixed_third
```

```python
import functools

import jax
import jax.numpy as jnp
from jax import lax
from jax.experimental import pallas as pl
from jax.experimental.pallas import tpu as pltpu
from jax.sharding import PartitionSpec as P

NT = 2
SWEEPS = 8
ITERS = 4
NMAT = 8
SPAN_X = 4
SPAN = 128
SUB = 8
TURN = SPAN // SUB

p_robin = 1.5
dt_coarse = 0.5
rho_bound = 0.9

RHO2 = rho_bound**2
SHIFT = 1.0 - RHO2
QUAD = RHO2 * RHO2 / 4.0 + SHIFT
Y_ONE = 2.0 / RHO2 - 1.0
GAIN = 128.0 / (RHO2**4 * (8.0 * Y_ONE**4 - 8.0 * Y_ONE**2 + 1.0))

F32 = jnp.float32
FIELD = (TURN, SPAN_X, SUB, SPAN)
PLANE = (NT, TURN, SUB, SPAN)


def stride_rows(row):
    return pl.ds(row, SUB, stride=TURN)


def lanes():
    return lax.broadcasted_iota(jnp.int32, (SUB, SPAN), 1)


def sublanes():
    return lax.broadcasted_iota(jnp.int32, (SUB, SPAN), 0)


def harmonic(left_k, right_k):
    return 2.0 * left_k * right_k / (left_k + right_k)


def pick(bits, table_ref):
    level = [table_ref[i] for i in range(NMAT)]
    for bit in bits:
        level = [jnp.where(bit, level[2 * i + 1], level[2 * i]) for i in range(len(level) // 2)]
    return level[0]


def up_z(value):
    return pltpu.roll(value, SPAN - 1, 1)


def down_z(value):
    return pltpu.roll(value, 1, 1)


def up_y(value):
    return pltpu.roll(value, SUB - 1, 0)


def down_y(value):
    return pltpu.roll(value, 1, 0)


def prepare(steps, initial, material, conduct, capacity, cx, cy, cz, weight, scale, start, kcell):
    lane, sub = lanes(), sublanes()
    inverse_h = (steps.astype(F32)) * (1.0 / dt_coarse)
    for j in range(TURN):
        for x in range(SPAN_X):
            mat = material[x, stride_rows(j), :]
            bits = [(mat & 1) != 0, (mat & 2) != 0, (mat & 4) != 0]
            kcell[j, x] = pick(bits, conduct)
            start[j, x] = pick(bits, capacity)
    for j in range(TURN):
        for x in range(SPAN_X):
            here = kcell[j, x]
            if x < SPAN_X - 1:
                cx[j, x] = harmonic(here, kcell[j, x + 1])
            if j < TURN - 1:
                cy[j, x] = harmonic(here, kcell[j + 1, x])
            else:
                cy[j, x] = jnp.where(sub < SUB - 1, harmonic(here, up_y(kcell[0, x])), 0.0)
            cz[j, x] = jnp.where(lane < SPAN - 1, harmonic(here, up_z(here)), 0.0)
    for j in range(TURN):
        for x in range(SPAN_X):
            base = cz[j, x] + down_z(cz[j, x]) + cy[j, x]
            base = base + (cy[j - 1, x] if j > 0 else down_y(cy[TURN - 1, x]))
            if x < SPAN_X - 1:
                base = base + cx[j, x]
            if x > 0:
                base = base + cx[j, x - 1]
            if x in (0, SPAN_X - 1):
                base = base + p_robin
            base = base + jnp.where((lane == 0) | (lane == SPAN - 1), p_robin, 0.0)
            if j == 0:
                base = base + jnp.where(sub == 0, p_robin, 0.0)
            if j == TURN - 1:
                base = base + jnp.where(sub == SUB - 1, p_robin, 0.0)
            diagonal = start[j, x] * inverse_h + base
            root = lax.rsqrt(diagonal)
            root = root * (1.5 - 0.5 * diagonal * root * root)
            scale[j, x] = root
            weight[j, x] = -base * root * root
            start[j, x] = initial[x, stride_rows(j), :] * (diagonal * root)
    for j in range(TURN):
        for x in range(SPAN_X):
            here = scale[j, x]
            if x < SPAN_X - 1:
                cx[j, x] = cx[j, x] * here * scale[j, x + 1]
            after = scale[j + 1, x] if j < TURN - 1 else up_y(scale[0, x])
            cy[j, x] = cy[j, x] * here * after
            cz[j, x] = cz[j, x] * here * up_z(here)


def couple(cx, cy, cz, source, emit):
    last = [cy[TURN - 1, x] * source[TURN - 1, x] for x in range(SPAN_X)]
    before = [down_y(value) for value in last]
    here = [source[0, x] for x in range(SPAN_X)]
    first = here
    for j in range(TURN):
        if j < TURN - 1:
            after = [source[j + 1, x] for x in range(SPAN_X)]
        else:
            after = [up_y(value) for value in first]
        side = [cx[j, x] for x in range(SPAN_X - 1)]
        total, following = [], []
        for x in range(SPAN_X):
            link = cy[j, x]
            value = before[x] + link * after[x]
            following.append(link * here[x])
            link = cz[j, x]
            value = value + link * up_z(here[x])
            value = value + down_z(link * here[x])
            if x < SPAN_X - 1:
                value = value + side[x] * here[x + 1]
            if x > 0:
                value = value + side[x - 1] * here[x - 1]
            total.append(value)
        emit(j, here, total)
        before, here = following, after


def kernel(first, final, *refs):
    refs = list(refs)
    take = lambda n: [refs.pop(0) for _ in range(n)]
    (substeps,) = take(1)
    if first:
        initial, material, conduct, capacity, trace_x = take(5)
    else:
        cx, cy, cz, weight, scale, start, face_a, face_b, come_y, come_z = take(10)
    trace_y, trace_z = take(2)
    if first:
        cx, cy, cz, weight, scale, start = take(6)
    if final:
        (field_out,) = take(1)
    out_a, out_b, out_y, out_z = take(4)
    if first:
        kcell, face_a, face_b = take(3)
    field, load, res, one, two, three = take(6)
    rows_z, cols_z, sum_z, turn_z, sum_a, sum_b = take(6)

    steps = substeps[0]
    place_x, place_y, place_z = (lax.axis_index("gx"), lax.axis_index("gy"), lax.axis_index("gz"))
    odd = place_x % 2
    plane_a = (SPAN_X - 1) * (1 - odd)
    plane_b = (SPAN_X - 1) * odd
    edge = (place_x == 0) | (place_x == lax.axis_size("gx") - 1)
    part = jnp.where(steps == 2, F32(p_robin), F32(2.0 * p_robin))
    part_b = jnp.where(edge, F32(0.0), part)
    sign_b = jnp.where(edge, F32(1.0), F32(-1.0))
    lane, sub = lanes(), sublanes()

    if first:
        prepare(steps, initial, material, conduct, capacity, cx, cy, cz, weight, scale, start, kcell)
        for n in range(NT):
            for j in range(TURN):
                face_a[n, j] = trace_x[1 - odd, n, stride_rows(j), :]
                face_b[n, j] = trace_x[odd, n, stride_rows(j), :]

    rows_z[...] = jnp.zeros((SPAN, SPAN), F32)
    for n in range(NT):
        for x in range(SPAN_X):
            row = 2 * (SPAN_X * n + x)
            if first:
                rows_z[pl.ds(row, 1), :] = trace_z[n, 1, pl.ds(x, 1), :]
                rows_z[pl.ds(row + 1, 1), :] = trace_z[n, 0, pl.ds(x, 1), :]
            else:
                rows_z[pl.ds(row + place_z, 1), :] = come_z[n, pl.ds(x, 1), :]
                rows_z[pl.ds(row + 1 - place_z, 1), :] = trace_z[n, place_z, pl.ds(x, 1), :]
    cols_z[...] = rows_z[...].T
    for j in range(TURN):
        sum_z[j] = jnp.zeros((SUB, SPAN), F32)
        for x in range(SPAN_X):
            field[j, x] = start[j, x]

    def coarse(n, carry):
        for j in range(TURN):
            column = cols_z[stride_rows(j), :]
            for x in range(SPAN_X):
                turned = pltpu.roll(column, SPAN - 1 - 2 * x - 2 * SPAN_X * n, 1)
                value = jnp.where((lane == 0) | (lane == SPAN - 1), turned, 0.0)
                if j in (0, TURN - 1):
                    side = 0 if j == 0 else 1
                    kept = trace_y[n, x, pl.ds(side, 1), :]
                    if not first:
                        come = come_y[n, pl.ds(x, 1), :]
                        kept = jnp.where(place_y == side, kept, come)
                    at = 0 if j == 0 else SUB - 1
                    value = value + jnp.where(sub == at, kept, 0.0)
                load[j, x] = value * scale[j, x]
        for j in range(TURN):
            data = face_a[n, j]
            load[j, plane_a] = load[j, plane_a] + data * scale[j, plane_a]
            sum_a[j] = -data
            data = face_b[n, j]
            load[j, plane_b] = load[j, plane_b] + data * scale[j, plane_b]
            sum_b[j] = sign_b * data
        for x in range(SPAN_X):
            kept = trace_y[n, x, pl.ds(1 - place_y, 1), :] if first else come_y[n, pl.ds(x, 1), :]
            out_y[n, pl.ds(x, 1), :] = -kept

        def substep(_, carry):
            def to_res(j, here, total):
                for x in range(SPAN_X):
                    res[j, x] = total[x] + weight[j, x] * here[x] + load[j, x]

            def to_one(j, here, total):
                for x in range(SPAN_X):
                    one[j, x] = total[x] + here[x]

            def plain(target):
                def emit(j, here, total):
                    for x in range(SPAN_X):
                        target[j, x] = total[x]

                return emit

            def mixed(target, other, factor):
                def emit(j, here, total):
                    for x in range(SPAN_X):
                        target[j, x] = total[x] + factor * other[j, x]

                return emit

            def close(j, here, total):
                mask_z = lane // 2
                gathered = None
                for x in range(SPAN_X):
                    value = field[j, x] + GAIN * (total[x] + QUAD * res[j, x])
                    field[j, x] = value
                    value = value * scale[j, x]
                    turned = pltpu.roll(value, 1 + 2 * x + 2 * SPAN_X * n, 1)
                    chosen = jnp.where(mask_z == SPAN_X * n + x, turned, 0.0)
                    gathered = chosen if gathered is None else gathered + chosen
                    if j in (0, TURN - 1):
                        side = 0 if j == 0 else 1
                        at = 0 if j == 0 else SUB - 1

                        @pl.when(place_y != side)
                        def _():
                            line = out_y[n, pl.ds(x, 1), :]
                            out_y[n, pl.ds(x, 1), :] = line + part * value[at : at + 1, :]

                sum_z[j] = sum_z[j] + part * gathered
                sum_a[j] = sum_a[j] + part * (field[j, plane_a] * scale[j, plane_a])
                sum_b[j] = sum_b[j] + part_b * (field[j, plane_b] * scale[j, plane_b])

            couple(cx, cy, cz, field, to_res)
            couple(cx, cy, cz, res, to_one)
            couple(cx, cy, cz, one, plain(two))
            couple(cx, cy, cz, two, mixed(res, one, SHIFT))
            couple(cx, cy, cz, res, plain(one))
            couple(cx, cy, cz, one, mixed(two, res, -RHO2))
            couple(cx, cy, cz, two, plain(three))
            couple(cx, cy, cz, three, close)
            return carry

        lax.fori_loop(0, steps, substep, 0)
        for j in range(TURN):
            if final:
                out_a[n, stride_rows(j), :] = sum_a[j]
                out_b[n, stride_rows(j), :] = sum_b[j]
            else:
                out_a[n, j] = sum_a[j]
                out_b[n, j] = sum_b[j]
        return carry

    lax.fori_loop(0, NT, coarse, 0)

    for j in range(TURN):
        turn_z[stride_rows(j), :] = sum_z[j]
    cols_z[...] = turn_z[...].T
    for n in range(NT):
        for x in range(SPAN_X):
            row = 2 * (SPAN_X * n + x) + place_z
            out_z[n, pl.ds(x, 1), :] = cols_z[pl.ds(row, 1), :] - rows_z[pl.ds(row, 1), :]
    if final:
        for j in range(TURN):
            for x in range(SPAN_X):
                field_out[x, stride_rows(j), :] = field[j, x] * scale[j, x]


def solve(first, final, *operands):
    vmem = pl.BlockSpec(memory_space=pltpu.VMEM)
    smem = pl.BlockSpec(memory_space=pltpu.SMEM)
    if first:
        in_specs = [smem, vmem, vmem, smem, smem] + [vmem] * 3
    else:
        in_specs = [smem] + [vmem] * 12
    shapes = []
    if first:
        shapes += [(TURN, SPAN_X - 1, SUB, SPAN)] + [FIELD] * 5
    if final:
        shapes += [(SPAN_X, SPAN, SPAN)]
    shapes += [(NT, SPAN, SPAN) if final else PLANE] * 2
    shapes += [(NT, SPAN_X, SPAN)] * 2
    scratch = ([FIELD, PLANE, PLANE] if first else []) + [FIELD] * 6
    scratch += [(SPAN, SPAN), (SPAN, SPAN), (TURN, SUB, SPAN), (SPAN, SPAN), (TURN, SUB, SPAN), (TURN, SUB, SPAN)]
    return pl.pallas_call(
        functools.partial(kernel, first, final),
        out_shape=[jax.ShapeDtypeStruct(shape, F32) for shape in shapes],
        in_specs=in_specs,
        out_specs=[vmem] * len(shapes),
        scratch_shapes=[pltpu.VMEM(shape, F32) for shape in scratch],
        compiler_params=pltpu.CompilerParams(vmem_limit_bytes=24 * 1024 * 1024),
    )(*operands)


def exchange(out_a, out_b, out_y, out_z):
    count = lax.axis_size("gx")
    pairs_a = [(i, i ^ 1) for i in range(count)]
    pairs_b = [(0, 0)] + [(i, i + 1 if i % 2 else i - 1) for i in range(1, count - 1)] + [(count - 1, count - 1)]
    swap = [(0, 1), (1, 0)]
    return (
        lax.ppermute(out_a, "gx", pairs_a),
        lax.ppermute(out_b, "gx", pairs_b),
        lax.ppermute(out_y, "gy", swap),
        lax.ppermute(out_z, "gz", swap),
    )


def local(initial, material, conduct, capacity, substeps, trace_x, trace_y, trace_z):
    steps = substeps.reshape(1)
    odd = lax.axis_index("gx") % 2
    place_y, place_z = (lax.axis_index("gy"), lax.axis_index("gz"))
    results = solve(True, False, steps, initial, material, conduct, capacity, trace_x, trace_y, trace_z)
    prepared, sent = results[:6], results[6:]
    for iteration in range(1, ITERS):
        arrived = exchange(*sent)
        final = iteration == ITERS - 1
        sent = solve(False, final, steps, *prepared, *arrived, trace_y, trace_z)
    field, *sent = sent
    face_a, face_b, come_y, come_z = exchange(*sent)
    got_x = jnp.stack([jnp.where(odd == 1, face_a, face_b), jnp.where(odd == 1, face_b, face_a)], 0)
    got_y = jnp.stack([jnp.where(place_y == side, trace_y[:, :, side], come_y) for side in range(2)], 2)
    got_z = jnp.stack([jnp.where(place_z == side, trace_z[:, side], come_z) for side in range(2)], 1)
    return (field, got_x, got_y, got_z)


def solution(mesh):
    placed = (
        P("gx", "gy", "gz"),
        P("gx", "gy", "gz"),
        P(),
        P(),
        P("gx", "gy", "gz"),
        P("gx", None, "gy", "gz"),
        P(None, "gx", "gy", "gz"),
        P(None, "gz", "gx", "gy"),
    )
    return jax.shard_map(
        local,
        mesh=mesh,
        in_specs=placed,
        out_specs=(
            P("gx", "gy", "gz"),
            P("gx", None, "gy", "gz"),
            P(None, "gx", "gy", "gz"),
            P(None, "gz", "gx", "gy"),
        ),
        check_vma=False,
    )
```

```python
import functools

import jax
import jax.numpy as jnp
from jax import lax
from jax.experimental import pallas as pl
from jax.experimental.pallas import tpu as pltpu
from jax.sharding import PartitionSpec as P

NT = 2
SWEEPS = 8
ITERS = 4
NMAT = 8
SPAN_X = 4
SPAN = 128
HALF = SPAN // 2
SUB = 8
TURN = 8

p_robin = 1.5
dt_coarse = 0.5
rho_bound = 0.9

RHO2 = rho_bound**2
SHIFT = 1.0 - RHO2
QUAD = RHO2 * RHO2 / 4.0 + SHIFT
Y_ONE = 2.0 / RHO2 - 1.0
GAIN = 128.0 / (RHO2**4 * (8.0 * Y_ONE**4 - 8.0 * Y_ONE**2 + 1.0))

F32 = jnp.float32
TILES = [(x, z) for x in range(SPAN_X) for z in range(2)]
ROWS = TURN * len(TILES) * SUB
ROWS_X = TURN * (SPAN_X - 1) * 2 * SUB
ROWS_A = TURN * 2 * SUB


def at(j, x, z):
    return pl.ds(((j * SPAN_X + x) * 2 + z) * SUB, SUB)


def at_x(j, x, z):
    return pl.ds(((j * (SPAN_X - 1) + x) * 2 + z) * SUB, SUB)


def at_face(n, j, z):
    return pl.ds(pl.multiple_of(((n * TURN + j) * 2 + z) * SUB, SUB), SUB)


def aligned(rows):
    return pl.ds(pl.multiple_of(rows, SUB), SUB)


def lanes():
    return lax.broadcasted_iota(jnp.int32, (SUB, SPAN), 1)


def sublanes():
    return lax.broadcasted_iota(jnp.int32, (SUB, SPAN), 0)


def harmonic(left_k, right_k):
    return 2.0 * left_k * right_k / (left_k + right_k)


def pick(bits, table_ref):
    level = [table_ref[i] for i in range(NMAT)]
    for bit in bits:
        level = [jnp.where(bit, level[2 * i + 1], level[2 * i]) for i in range(len(level) // 2)]
    return level[0]


def up_z(value):
    return pltpu.roll(value, SPAN - 1, 1)


def down_z(value):
    return pltpu.roll(value, 1, 1)


def other_half(value):
    return pltpu.roll(value, HALF, 1)


def up_y(value):
    turned = pltpu.roll(value, SUB - 1, 0)
    return jnp.where(sublanes() < SUB - 1, turned, other_half(turned))


def down_y(value):
    turned = pltpu.roll(value, 1, 0)
    return jnp.where(sublanes() > 0, turned, other_half(turned))


def pairing(back):
    row = lax.broadcasted_iota(jnp.int32, (2 * SPAN, 2 * SPAN), 1 if back else 0)
    col = lax.broadcasted_iota(jnp.int32, (2 * SPAN, 2 * SPAN), 0 if back else 1)
    half, z = row // SPAN, row % SPAN
    place = (z % 2) * SPAN + half * HALF + z // 2
    return jnp.where(col == place, 1.0, 0.0).astype(jnp.bfloat16)


def moved(value, matrix, narrow=False):
    dot = functools.partial(jnp.dot, preferred_element_type=F32)
    high = value.astype(jnp.bfloat16)
    if narrow:
        return dot(high, matrix)
    rest = value - high.astype(F32)
    middle = rest.astype(jnp.bfloat16)
    low = (rest - middle.astype(F32)).astype(jnp.bfloat16)
    return dot(high, matrix) + (dot(middle, matrix) + dot(low, matrix))


def rows_of(j, half):
    return pl.ds(HALF * half + j, SUB, stride=TURN)


def split(planes, matrix, narrow=False):
    pieces = []
    for ref, lead in planes:
        for j in range(TURN):
            halves = [ref[(*lead, rows_of(j, half), slice(None))].astype(F32) for half in range(2)]
            pieces.append(jnp.concatenate(halves, 1))
    out = moved(jnp.concatenate(pieces, 0), matrix, narrow)

    def tile(plane, j, z):
        row = (plane * TURN + j) * SUB
        return out[row : row + SUB, z * SPAN : (z + 1) * SPAN]

    return tile


def join(planes, matrix):
    pieces = [jnp.concatenate(tiles[j], 1) for _, _, tiles in planes for j in range(TURN)]
    out = moved(jnp.concatenate(pieces, 0), matrix)
    for plane, (ref, lead, _) in enumerate(planes):
        for j in range(TURN):
            row = (plane * TURN + j) * SUB
            for half in range(2):
                ref[(*lead, rows_of(j, half), slice(None))] = out[row : row + SUB, half * SPAN : (half + 1) * SPAN]


def prepare(steps, matrix, arrive, initial, material, conduct, capacity, cx, cy, cw, cz, weight, scale, start, kcell):
    lane, sub = lanes(), sublanes()
    inverse_h = steps.astype(F32) * (1.0 / dt_coarse)
    tiles = split([(material, (x,)) for x in range(SPAN_X)], matrix, narrow=True)
    for j in range(TURN):
        for x in range(SPAN_X):
            for z in range(2):
                mat = tiles(x, j, z).astype(jnp.int32)
                bits = [(mat & 1) != 0, (mat & 2) != 0, (mat & 4) != 0]
                kcell[at(j, x, z), :] = pick(bits, conduct)
                start[at(j, x, z), :] = pick(bits, capacity)
    inner = (lane != HALF - 1) & (lane != SPAN - 1)
    for j in range(TURN):
        for x, z in TILES:
            here = kcell[at(j, x, z), :]
            if x < SPAN_X - 1:
                cx[at_x(j, x, z), :] = harmonic(here, kcell[at(j, x + 1, z), :])
            if j < TURN - 1:
                cy[at(j, x, z), :] = harmonic(here, kcell[at(j + 1, x, z), :])
            else:
                link = harmonic(here, up_y(kcell[at(0, x, z), :]))
                cy[at(j, x, z), :] = jnp.where((sub == SUB - 1) & (lane >= HALF), 0.0, link)
            if z == 0:
                cz[at(j, x, z), :] = harmonic(here, kcell[at(j, x, 1), :])
            else:
                cz[at(j, x, z), :] = jnp.where(inner, harmonic(here, up_z(kcell[at(j, x, 0), :])), 0.0)
    for j in range(TURN):
        for x, z in TILES:
            base = cz[at(j, x, 0), :] + (cz[at(j, x, 1), :] if z else down_z(cz[at(j, x, 1), :]))
            base = base + cy[at(j, x, z), :]
            base = base + (cy[at(j - 1, x, z), :] if j > 0 else down_y(cy[at(TURN - 1, x, z), :]))
            if x < SPAN_X - 1:
                base = base + cx[at_x(j, x, z), :]
            if x > 0:
                base = base + cx[at_x(j, x - 1, z), :]
            if x in (0, SPAN_X - 1):
                base = base + p_robin
            end = HALF - 1 if z else 0
            base = base + jnp.where((lane == end) | (lane == end + HALF), p_robin, 0.0)
            if j == 0:
                base = base + jnp.where((sub == 0) & (lane < HALF), p_robin, 0.0)
            if j == TURN - 1:
                base = base + jnp.where((sub == SUB - 1) & (lane >= HALF), p_robin, 0.0)
            diagonal = start[at(j, x, z), :] * inverse_h + base
            root = lax.rsqrt(diagonal)
            root = root * (1.5 - 0.5 * diagonal * root * root)
            scale[at(j, x, z), :] = root
            weight[at(j, x, z), :] = -base * root * root
            start[at(j, x, z), :] = diagonal * root
    for j in range(TURN):
        for x, z in TILES:
            here = scale[at(j, x, z), :]
            if x < SPAN_X - 1:
                cx[at_x(j, x, z), :] = cx[at_x(j, x, z), :] * here * scale[at(j, x + 1, z), :]
            after = scale[at(j + 1, x, z), :] if j < TURN - 1 else up_y(scale[at(0, x, z), :])
            cy[at(j, x, z), :] = cy[at(j, x, z), :] * here * after
            beside = up_z(scale[at(j, x, 0), :]) if z else scale[at(j, x, 1), :]
            cz[at(j, x, z), :] = cz[at(j, x, z), :] * here * beside
    for x, z in TILES:
        cw[at(0, x, z), :] = down_y(cy[at(TURN - 1, x, z), :])
    arrive(1)
    tiles = split([(initial, (x,)) for x in range(SPAN_X)], matrix)
    for j in range(TURN):
        for x, z in TILES:
            start[at(j, x, z), :] = start[at(j, x, z), :] * tiles(x, j, z)


def couple(cx, cy, cw, cz, begin, source, emit):
    def load(j):
        return {p: source[at(j, *p), :] for p in TILES}

    def wrap_down(row):
        return {p: cw[at(0, *p), :] * down_y(row[p]) for p in TILES}

    here = load(begin)
    before = load((begin - 1) % TURN)
    if begin == 0:
        before = wrap_down(before)
    else:
        before = {p: cy[at(begin - 1, *p), :] * before[p] for p in TILES}
    for turn in range(TURN):
        j = (begin + turn) % TURN
        following = load((j + 1) % TURN)
        after = following if j < TURN - 1 else {p: up_y(following[p]) for p in TILES}
        total, later = {}, {}
        for p in TILES:
            link = cy[at(j, *p), :]
            total[p] = before[p] + link * after[p]
            if j < TURN - 1:
                later[p] = link * here[p]
        for x in range(SPAN_X):
            even, odd = (x, 0), (x, 1)
            link = cz[at(j, *even), :]
            total[even] = total[even] + link * here[odd]
            total[odd] = total[odd] + link * here[even]
            link = cz[at(j, *odd), :]
            total[odd] = total[odd] + link * up_z(here[even])
            total[even] = total[even] + down_z(link * here[odd])
        for x in range(SPAN_X - 1):
            for z in range(2):
                link = cx[at_x(j, x, z), :]
                total[(x, z)] = total[(x, z)] + link * here[(x + 1, z)]
                total[(x + 1, z)] = total[(x + 1, z)] + link * here[(x, z)]
        emit(j, here, total)
        before = later if j < TURN - 1 else wrap_down(here)
        here = following


def kernel(first, final, *refs):
    refs = list(refs)
    take = lambda n: [refs.pop(0) for _ in range(n)]
    if first:
        far = take(8)
        cx, cy, cw, cz, weight, scale, start, keep_x, keep_y, keep_z = take(10)
    else:
        (substeps,) = take(1)
        cx, cy, cw, cz, weight, scale, start, keep_x, keep_y, keep_z = take(10)
        face_low, face_high, come_y, come_z = take(4)
    if final:
        (field_out,) = take(1)
    out_low, out_high, out_y, out_z = take(4)
    if first:
        kcell, face_low, face_high, come_y, come_z = take(5)
        near = take(8)
        (arrivals,) = take(1)
    field, old, load, res, one, two, three = take(7)
    near_links, far_links = take(4), (cx, cy, cz, weight)
    if not first:
        for source, target in zip(far_links, near_links):
            target[...] = source[...]
    cx, cy, cz, weight = near_links
    lines, spare, turned_z, cols_z, sum_z = take(5)

    place_x, place_y, place_z = (lax.axis_index("gx"), lax.axis_index("gy"), lax.axis_index("gz"))
    ends_x = (place_x == 0, place_x == lax.axis_size("gx") - 1)
    lane, sub = lanes(), sublanes()

    if first:
        order = (2, 3, 4, 1, 0, 5, 6, 7)
        copies = {i: pltpu.make_async_copy(far[i], near[i], arrivals.at[i]) for i in order}
        for i in order:
            copies[i].start()
        initial, material, conduct, capacity, substeps, trace_x, trace_y, trace_z = near
        matrix = pairing(False)
        for i in (2, 3, 4, 1):
            copies[i].wait()
        steps = substeps[0]
        prepare(
            steps, matrix, lambda _: copies[0].wait(),
            initial, material, conduct, capacity, cx, cy, cw, cz, weight, scale, start, kcell,
        )
        for source, target in zip(near_links, far_links):
            target[...] = source[...]
        for i in (5, 6, 7):
            copies[i].wait()
        low_tiles, high_tiles = [split([(trace_x, (side, n)) for n in range(NT)], matrix) for side in range(2)]
        for n in range(NT):
            for j in range(TURN):
                for z in range(2):
                    tile = at_face(n, j, z)
                    face_low[tile, :] = low_tiles(n, j, z)
                    face_high[tile, :] = high_tiles(n, j, z)
                    keep_x[tile, :] = jnp.where(ends_x[0], low_tiles(n, j, z), high_tiles(n, j, z))
        for n in range(NT):
            for x in range(SPAN_X):
                keep_z[n, pl.ds(x, 1), :] = trace_z[n, place_z, pl.ds(x, 1), :]
                come_z[n, pl.ds(x, 1), :] = trace_z[n, 1 - place_z, pl.ds(x, 1), :]
                for side in range(2):
                    spare[pl.ds(SUB * side + SPAN_X * n + x, 1), :] = trace_y[n, x, pl.ds(side, 1), :]
        both = spare[pl.ds(0, 2 * SUB), :]
        both = moved(jnp.concatenate([both, both], 1), matrix)
        for z in range(2):
            spare[pl.ds(2 * SUB * (z + 1), 2 * SUB), :] = both[:, z * SPAN : (z + 1) * SPAN]
        for n in range(NT):
            for i, (x, z) in enumerate(TILES):
                row = SPAN_X * n + x + 2 * SUB * (z + 1)
                keep_y[pl.ds(SUB * n + i, 1), :] = spare[pl.ds(row + SUB * place_y, 1), :]
                come_y[pl.ds(SUB * n + i, 1), :] = spare[pl.ds(row + SUB * (1 - place_y), 1), :]
    else:
        steps = substeps[0]
    last_part = jnp.where(steps == 2, F32(p_robin), F32(2.0 * p_robin))
    mid_part = jnp.where(steps == 2, F32(p_robin), F32(0.0))
    faces_x = ((0, face_low, out_low), (SPAN_X - 1, face_high, out_high))

    turned_z[...] = jnp.zeros((SPAN, SPAN), F32)
    inner_z = 1 - place_z
    for n in range(NT):
        for x in range(SPAN_X):
            row = 2 * (SPAN_X * n + x)
            for side, data in ((inner_z, come_z), (place_z, keep_z)):
                line = data[n, pl.ds(x, 1), :]
                place = row + (HALF - 1) * side
                turned_z[pl.ds(place, 1), :] = line
                turned_z[pl.ds((place + HALF) % SPAN, 1), :] = line
    cols_z[...] = turned_z[...].T
    outer_lanes = (lane < HALF // 2) | (lane >= SPAN - HALF // 2)
    low_half = outer_lanes == (lane % 2 == 0)
    for j in range(TURN):
        value = jnp.where(low_half, cols_z[rows_of(j, 0), :], cols_z[rows_of(j, 1), :])
        turned_z[pl.ds(SUB * j, SUB), :] = value
        sum_z[pl.ds(SUB * j, SUB), :] = jnp.zeros((SUB, SPAN), F32)
    for j in range(TURN):
        for p in TILES:
            value = start[at(j, *p), :]
            field[at(j, *p), :] = value
    end_even = (lane == 0) | (lane == HALF)
    end_odd = (lane == HALF - 1) | (lane == SPAN - 1)
    corner_low = (sub == 0) & (lane < HALF)
    corner_high = (sub == SUB - 1) & (lane >= HALF)

    if final:
        back = pairing(True)

    def coarse(n, nothing):
        tile_y = aligned(SUB * n)
        kept, come = keep_y[tile_y, :], come_y[tile_y, :]
        lines[pl.ds(0, SUB), :] = jnp.where(place_y == 0, kept, come)
        lines[pl.ds(SUB, SUB), :] = jnp.where(place_y == 0, come, kept)
        for j in range(TURN):
            column = turned_z[pl.ds(SUB * j, SUB), :]
            for x in range(SPAN_X):
                around = pltpu.roll(column, (SPAN - 2 * x - 2 * SPAN_X * n) % SPAN, 1)
                for z, ends in enumerate((end_even, end_odd)):
                    value = jnp.where(ends, around, 0.0)
                    line = 2 * x + z
                    if j == 0:
                        value = value + jnp.where(corner_low, lines[pl.ds(line, 1), :], 0.0)
                    if j == TURN - 1:
                        value = value + jnp.where(corner_high, lines[pl.ds(SUB + line, 1), :], 0.0)
                    load[at(j, x, z), :] = value * scale[at(j, x, z), :]
        for j in range(TURN):
            for z in range(2):
                tile = at_face(n, j, z)
                for end, (x, data, _) in zip(ends_x, faces_x):
                    value = jnp.where(end, keep_x[tile, :], data[tile, :])
                    load[at(j, x, z), :] = load[at(j, x, z), :] + value * scale[at(j, x, z), :]

        def substep(index, nothing):
            def to_res(j, here, total):
                for p in TILES:
                    tile = at(j, *p)
                    old[tile, :] = here[p]
                    res[tile, :] = total[p] + weight[tile, :] * here[p] + load[tile, :]

            def to_one(j, here, total):
                for p in TILES:
                    one[at(j, *p), :] = total[p] + here[p]

            def plain(out):
                def emit(j, here, total):
                    for p in TILES:
                        out[at(j, *p), :] = total[p]

                return emit

            def mixed(out, other, factor):
                def emit(j, here, total):
                    for p in TILES:
                        tile = at(j, *p)
                        out[tile, :] = total[p] + factor * other[tile, :]

                return emit

            def close(j, here, total):
                for p in TILES:
                    tile = at(j, *p)
                    field[tile, :] = old[tile, :] + GAIN * (total[p] + QUAD * res[tile, :])

            go = functools.partial(couple, cx, cy, cw, cz)
            go(0, field, to_res)
            go(1, res, to_one)
            go(2, one, plain(two))
            go(3, two, mixed(res, one, SHIFT))
            go(4, res, plain(one))
            go(5, one, mixed(two, res, -RHO2))
            go(6, two, plain(three))
            go(7, three, close)
            return nothing

        lax.fori_loop(0, steps, substep, 0)

        def mean(start_row, last, mid, step=1):
            if step == 1:
                rows = aligned(start_row)
            else:
                rows = pl.ds(start_row, SUB, stride=step)
            return scale[rows, :] * (last * field[rows, :] + mid * old[rows, :])

        planes = []
        for x, data, out in faces_x:
            made = []
            for j in range(TURN):
                pair = []
                for z in range(2):
                    tile = at_face(n, j, z)
                    pair.append(mean(at(j, x, z).start, last_part, mid_part) - data[tile, :])
                    if not final:
                        out[tile, :] = pair[z]
                made.append(pair)
            planes.append((out, (n,), made))
        if final:
            join(planes, back)
        for j in range(TURN):
            gathered = sum_z[pl.ds(SUB * j, SUB), :]
            for x in range(SPAN_X):
                value = mean(at(j, x, 0).start + SUB * inner_z, last_part, mid_part)
                shift = 2 * x + 2 * SPAN_X * n
                mine = (lane - (HALF - 1) * inner_z - shift) % HALF == 0
                gathered = gathered + jnp.where(mine, pltpu.roll(value, shift, 1), 0.0)
            sum_z[pl.ds(SUB * j, SUB), :] = gathered
        corner = jnp.where(place_y == 0, at(TURN - 1, 0, 0).start + SUB - 1, 0)
        value = mean(corner, last_part, mid_part, SUB) - come_y[tile_y, :]
        if final:
            value = jnp.where((lane >= HALF) == (place_y == 0), value, other_half(value))
            spare[tile_y, :] = value
        else:
            out_y[tile_y, :] = other_half(value)
        return nothing

    lax.fori_loop(0, NT, coarse, 0)

    for j in range(TURN):
        value = sum_z[pl.ds(SUB * j, SUB), :]
        for half in range(2):
            turned_z[rows_of(j, half), :] = value
    cols_z[...] = turned_z[...].T
    line_lane = lax.broadcasted_iota(jnp.int32, (1, SPAN), 1)
    for n in range(NT):
        for x in range(SPAN_X):
            place = 2 * (SPAN_X * n + x) + (HALF - 1) * inner_z
            low, high = cols_z[pl.ds(place, 1), :], cols_z[pl.ds((place + HALF) % SPAN, 1), :]
            out_z[n, pl.ds(x, 1), :] = jnp.where(line_lane < HALF, low, high) - come_z[n, pl.ds(x, 1), :]
    if final:
        even, odd_z = spare[pl.ds(0, SUB, stride=2), :], spare[pl.ds(1, SUB, stride=2), :]
        both = jnp.concatenate([even, odd_z], 1)
        spare[pl.ds(2 * SUB, 2 * SUB), :] = moved(jnp.concatenate([both, both], 0), back)[:, :SPAN]
        for n in range(NT):
            for x in range(SPAN_X):
                out_y[n, pl.ds(x, 1), :] = spare[pl.ds(2 * SUB + SPAN_X * n + x, 1), :]
        planes = []
        for x in range(SPAN_X):
            made = [[field[at(j, x, z), :] * scale[at(j, x, z), :] for z in range(2)] for j in range(TURN)]
            planes.append((field_out, (x,), made))
        join(planes, back)


def solve(first, final, *operands):
    vmem = pl.BlockSpec(memory_space=pltpu.VMEM)
    smem = pl.BlockSpec(memory_space=pltpu.SMEM)
    far = pl.BlockSpec(memory_space=pltpu.MemorySpace.HBM)
    wide = lambda rows: (rows, SPAN)
    lines_z = (NT, SPAN_X, SPAN)
    if first:
        in_specs = [far] * 8
    else:
        in_specs = [smem] + [vmem] * 14
    shapes = []
    if first:
        shapes += [wide(ROWS_X), wide(ROWS), wide(len(TILES) * SUB)] + [wide(ROWS)] * 4
        shapes += [wide(NT * ROWS_A), wide(NT * SUB), lines_z]
    if final:
        shapes += [(SPAN_X, SPAN, SPAN)]
    shapes += [(NT, SPAN, SPAN) if final else wide(NT * ROWS_A)] * 2
    shapes += [lines_z if final else wide(NT * SUB), lines_z]
    scratch = []
    if first:
        scratch += [pltpu.VMEM(wide(ROWS), F32)] + [pltpu.VMEM(wide(NT * ROWS_A), F32)] * 2
        scratch += [pltpu.VMEM(wide(NT * SUB), F32), pltpu.VMEM(lines_z, F32)]
        for i, operand in enumerate(operands):
            space = pltpu.SMEM if i in (2, 3, 4) else pltpu.VMEM
            scratch.append(space(operand.shape, operand.dtype))
        scratch.append(pltpu.SemaphoreType.DMA((8,)))
    scratch += [pltpu.VMEM(wide(ROWS), F32)] * 7
    scratch += [pltpu.VMEM(wide(ROWS_X), F32)] + [pltpu.VMEM(wide(ROWS), F32)] * 3
    scratch += [pltpu.VMEM(wide(2 * SUB), F32), pltpu.VMEM(wide(6 * SUB), F32)]
    scratch += [pltpu.VMEM(wide(SPAN), F32)] * 2 + [pltpu.VMEM(wide(TURN * SUB), F32)]
    return pl.pallas_call(
        functools.partial(kernel, first, final),
        out_shape=[jax.ShapeDtypeStruct(shape, F32) for shape in shapes],
        in_specs=in_specs,
        out_specs=[vmem] * len(shapes),
        scratch_shapes=scratch,
        compiler_params=pltpu.CompilerParams(vmem_limit_bytes=(52 if first else 24) * 1024 * 1024),
    )(*operands)


def exchange(out_low, out_high, out_y, out_z):
    count = lax.axis_size("gx")
    up = [(i, (i + 1) % count) for i in range(count)]
    down = [(j, i) for i, j in up]
    swap = [(0, 1), (1, 0)]
    return (
        lax.ppermute(out_high, "gx", up),
        lax.ppermute(out_low, "gx", down),
        lax.ppermute(out_y, "gy", swap),
        lax.ppermute(out_z, "gz", swap),
    )


def local(initial, material, conduct, capacity, substeps, trace_x, trace_y, trace_z):
    steps = substeps.reshape(1)
    place_x, place_y, place_z = (lax.axis_index("gx"), lax.axis_index("gy"), lax.axis_index("gz"))
    results = solve(True, False, initial, material, conduct, capacity, steps, trace_x, trace_y, trace_z)
    prepared, sent = results[:10], results[10:]
    for iteration in range(1, ITERS):
        arrived = exchange(*sent)
        final = iteration == ITERS - 1
        sent = solve(False, final, steps, *prepared, *arrived)
    field, *sent = sent
    face_low, face_high, come_y, come_z = exchange(*sent)
    face_low = jnp.where(place_x == 0, trace_x[0], face_low)
    face_high = jnp.where(place_x == lax.axis_size("gx") - 1, trace_x[1], face_high)
    got_x = jnp.stack([face_low, face_high], 0)
    got_y = jnp.stack([jnp.where(place_y == side, trace_y[:, :, side], come_y) for side in range(2)], 2)
    got_z = jnp.stack([jnp.where(place_z == side, trace_z[:, side], come_z) for side in range(2)], 1)
    return (field, got_x, got_y, got_z)


def solution(mesh):
    placed = (
        P("gx", "gy", "gz"),
        P("gx", "gy", "gz"),
        P(),
        P(),
        P("gx", "gy", "gz"),
        P("gx", None, "gy", "gz"),
        P(None, "gx", "gy", "gz"),
        P(None, "gz", "gx", "gy"),
    )
    return jax.shard_map(
        local,
        mesh=mesh,
        in_specs=placed,
        out_specs=(
            P("gx", "gy", "gz"),
            P("gx", None, "gy", "gz"),
            P(None, "gx", "gy", "gz"),
            P(None, "gz", "gx", "gy"),
        ),
        check_vma=False,
    )
```

```python
import functools

import jax
import jax.numpy as jnp
from jax import lax
from jax.experimental import pallas as pl
from jax.experimental.pallas import tpu as pltpu
from jax.sharding import PartitionSpec as P

NT = 2
SWEEPS = 8
ITERS = 4
NMAT = 8
SPAN_X = 4
SPAN = 128
HALF = SPAN // 2
SUB = 8
TURN = 8

p_robin = 1.5
dt_coarse = 0.5
rho_bound = 0.9

RHO2 = rho_bound**2
SHIFT = 1.0 - RHO2
QUAD = RHO2 * RHO2 / 4.0 + SHIFT
Y_ONE = 2.0 / RHO2 - 1.0
GAIN = 128.0 / (RHO2**4 * (8.0 * Y_ONE**4 - 8.0 * Y_ONE**2 + 1.0))

F32 = jnp.float32
TILES = [(x, z) for x in range(SPAN_X) for z in range(2)]
ROWS = TURN * len(TILES) * SUB
ROWS_X = TURN * (SPAN_X - 1) * 2 * SUB
ROWS_A = TURN * 2 * SUB


def at(j, x, z):
    return pl.ds(((j * SPAN_X + x) * 2 + z) * SUB, SUB)


def at_x(j, x, z):
    return pl.ds(((j * (SPAN_X - 1) + x) * 2 + z) * SUB, SUB)


def at_face(n, j, z):
    return pl.ds(pl.multiple_of(((n * TURN + j) * 2 + z) * SUB, SUB), SUB)


def aligned(rows):
    return pl.ds(pl.multiple_of(rows, SUB), SUB)


def lanes():
    return lax.broadcasted_iota(jnp.int32, (SUB, SPAN), 1)


def sublanes():
    return lax.broadcasted_iota(jnp.int32, (SUB, SPAN), 0)


def harmonic(left_k, right_k):
    return 2.0 * left_k * right_k / (left_k + right_k)


def pick(bits, table_ref):
    level = [table_ref[i] for i in range(NMAT)]
    for bit in bits:
        level = [jnp.where(bit, level[2 * i + 1], level[2 * i]) for i in range(len(level) // 2)]
    return level[0]


def up_z(value):
    return pltpu.roll(value, SPAN - 1, 1)


def down_z(value):
    return pltpu.roll(value, 1, 1)


def other_half(value):
    return pltpu.roll(value, HALF, 1)


def up_y(value):
    turned = pltpu.roll(value, SUB - 1, 0)
    return jnp.where(sublanes() < SUB - 1, turned, other_half(turned))


def down_y(value):
    turned = pltpu.roll(value, 1, 0)
    return jnp.where(sublanes() > 0, turned, other_half(turned))


def pairing(back):
    row = lax.broadcasted_iota(jnp.int32, (2 * SPAN, 2 * SPAN), 1 if back else 0)
    col = lax.broadcasted_iota(jnp.int32, (2 * SPAN, 2 * SPAN), 0 if back else 1)
    half, z = row // SPAN, row % SPAN
    place = (z % 2) * SPAN + half * HALF + z // 2
    return jnp.where(col == place, 1.0, 0.0).astype(jnp.bfloat16)


def moved(value, matrix, narrow=False):
    dot = functools.partial(jnp.dot, preferred_element_type=F32)
    high = value.astype(jnp.bfloat16)
    if narrow:
        return dot(high, matrix)
    rest = value - high.astype(F32)
    middle = rest.astype(jnp.bfloat16)
    low = (rest - middle.astype(F32)).astype(jnp.bfloat16)
    return dot(high, matrix) + (dot(middle, matrix) + dot(low, matrix))


def rows_of(j, half):
    return pl.ds(HALF * half + j, SUB, stride=TURN)


def split(planes, matrix, narrow=False):
    pieces = []
    for ref, lead in planes:
        for j in range(TURN):
            halves = [ref[(*lead, rows_of(j, half), slice(None))].astype(F32) for half in range(2)]
            pieces.append(jnp.concatenate(halves, 1))
    out = moved(jnp.concatenate(pieces, 0), matrix, narrow)

    def tile(plane, j, z):
        row = (plane * TURN + j) * SUB
        return out[row : row + SUB, z * SPAN : (z + 1) * SPAN]

    return tile


def join(planes, matrix):
    pieces = [jnp.concatenate(tiles[j], 1) for _, _, tiles in planes for j in range(TURN)]
    out = moved(jnp.concatenate(pieces, 0), matrix)
    for plane, (ref, lead, _) in enumerate(planes):
        for j in range(TURN):
            row = (plane * TURN + j) * SUB
            for half in range(2):
                ref[(*lead, rows_of(j, half), slice(None))] = out[row : row + SUB, half * SPAN : (half + 1) * SPAN]


def prepare(steps, matrix, arrive, initial, material, conduct, capacity, cx, cy, cw, cz, weight, scale, start, kcell):
    lane, sub = lanes(), sublanes()
    inverse_h = steps.astype(F32) * (1.0 / dt_coarse)
    tiles = split([(material, (x,)) for x in range(SPAN_X)], matrix, narrow=True)
    for j in range(TURN):
        for x in range(SPAN_X):
            for z in range(2):
                mat = tiles(x, j, z).astype(jnp.int32)
                bits = [(mat & 1) != 0, (mat & 2) != 0, (mat & 4) != 0]
                kcell[at(j, x, z), :] = pick(bits, conduct)
                start[at(j, x, z), :] = pick(bits, capacity)
    inner = (lane != HALF - 1) & (lane != SPAN - 1)
    for j in range(TURN):
        for x, z in TILES:
            here = kcell[at(j, x, z), :]
            if x < SPAN_X - 1:
                cx[at_x(j, x, z), :] = harmonic(here, kcell[at(j, x + 1, z), :])
            if j < TURN - 1:
                cy[at(j, x, z), :] = harmonic(here, kcell[at(j + 1, x, z), :])
            else:
                link = harmonic(here, up_y(kcell[at(0, x, z), :]))
                cy[at(j, x, z), :] = jnp.where((sub == SUB - 1) & (lane >= HALF), 0.0, link)
            if z == 0:
                cz[at(j, x, z), :] = harmonic(here, kcell[at(j, x, 1), :])
            else:
                cz[at(j, x, z), :] = jnp.where(inner, harmonic(here, up_z(kcell[at(j, x, 0), :])), 0.0)
    for j in range(TURN):
        for x, z in TILES:
            base = cz[at(j, x, 0), :] + (cz[at(j, x, 1), :] if z else down_z(cz[at(j, x, 1), :]))
            base = base + cy[at(j, x, z), :]
            base = base + (cy[at(j - 1, x, z), :] if j > 0 else down_y(cy[at(TURN - 1, x, z), :]))
            if x < SPAN_X - 1:
                base = base + cx[at_x(j, x, z), :]
            if x > 0:
                base = base + cx[at_x(j, x - 1, z), :]
            if x in (0, SPAN_X - 1):
                base = base + p_robin
            end = HALF - 1 if z else 0
            base = base + jnp.where((lane == end) | (lane == end + HALF), p_robin, 0.0)
            if j == 0:
                base = base + jnp.where((sub == 0) & (lane < HALF), p_robin, 0.0)
            if j == TURN - 1:
                base = base + jnp.where((sub == SUB - 1) & (lane >= HALF), p_robin, 0.0)
            diagonal = start[at(j, x, z), :] * inverse_h + base
            root = lax.rsqrt(diagonal)
            root = root * (1.5 - 0.5 * diagonal * root * root)
            scale[at(j, x, z), :] = root
            weight[at(j, x, z), :] = -base * root * root
            start[at(j, x, z), :] = diagonal * root
    for j in range(TURN):
        for x, z in TILES:
            here = scale[at(j, x, z), :]
            if x < SPAN_X - 1:
                cx[at_x(j, x, z), :] = cx[at_x(j, x, z), :] * here * scale[at(j, x + 1, z), :]
            after = scale[at(j + 1, x, z), :] if j < TURN - 1 else up_y(scale[at(0, x, z), :])
            cy[at(j, x, z), :] = cy[at(j, x, z), :] * here * after
            beside = up_z(scale[at(j, x, 0), :]) if z else scale[at(j, x, 1), :]
            cz[at(j, x, z), :] = cz[at(j, x, z), :] * here * beside
    for x, z in TILES:
        cw[at(0, x, z), :] = down_y(cy[at(TURN - 1, x, z), :])
    arrive(1)
    tiles = split([(initial, (x,)) for x in range(SPAN_X)], matrix)
    for j in range(TURN):
        for x, z in TILES:
            start[at(j, x, z), :] = start[at(j, x, z), :] * tiles(x, j, z)


def couple(cx, cy, cw, cz, begin, source, emit):
    def load(j):
        return {p: source[at(j, *p), :] for p in TILES}

    def wrap_down(row):
        return {p: cw[at(0, *p), :] * down_y(row[p]) for p in TILES}

    here = load(begin)
    before = load((begin - 1) % TURN)
    if begin == 0:
        before = wrap_down(before)
    else:
        before = {p: cy[at(begin - 1, *p), :] * before[p] for p in TILES}
    for turn in range(TURN):
        j = (begin + turn) % TURN
        following = load((j + 1) % TURN)
        after = following if j < TURN - 1 else {p: up_y(following[p]) for p in TILES}
        total, later = {}, {}
        for p in TILES:
            link = cy[at(j, *p), :]
            total[p] = before[p] + link * after[p]
            if j < TURN - 1:
                later[p] = link * here[p]
        for x in range(SPAN_X):
            even, odd = (x, 0), (x, 1)
            link = cz[at(j, *even), :]
            total[even] = total[even] + link * here[odd]
            total[odd] = total[odd] + link * here[even]
            link = cz[at(j, *odd), :]
            total[odd] = total[odd] + link * up_z(here[even])
            total[even] = total[even] + down_z(link * here[odd])
        for x in range(SPAN_X - 1):
            for z in range(2):
                link = cx[at_x(j, x, z), :]
                total[(x, z)] = total[(x, z)] + link * here[(x + 1, z)]
                total[(x + 1, z)] = total[(x + 1, z)] + link * here[(x, z)]
        emit(j, here, total)
        before = later if j < TURN - 1 else wrap_down(here)
        here = following


def kernel(first, final, *refs):
    refs = list(refs)
    take = lambda n: [refs.pop(0) for _ in range(n)]
    if first:
        far = take(8)
        cx, cy, cw, cz, weight, scale, start, keep_x, keep_y, keep_z = take(10)
    else:
        (substeps,) = take(1)
        cx, cy, cw, cz, weight, scale, start, keep_x, keep_y, keep_z = take(10)
        face_low, face_high, come_y, come_z = take(4)
    if final:
        (field_out,) = take(1)
    out_low, out_high, out_y, out_z = take(4)
    if first:
        kcell, face_low, face_high, come_y, come_z = take(5)
        near = take(8)
        (arrivals,) = take(1)
    field, old, load, res, one, two, three = take(7)
    near_links, far_links = take(4), (cx, cy, cz, weight)
    if not first:
        for source, target in zip(far_links, near_links):
            target[...] = source[...]
    cx, cy, cz, weight = near_links
    lines, spare, turned_z, cols_z, sum_z = take(5)

    place_x, place_y, place_z = (lax.axis_index("gx"), lax.axis_index("gy"), lax.axis_index("gz"))
    planes_x = ((SPAN_X - 1) * place_z, (SPAN_X - 1) * (1 - place_z))
    outer_x = [jnp.where(plane == 0, 0, lax.axis_size("gx") - 1) for plane in planes_x]
    ends_x = [place_x == outer for outer in outer_x]
    lane, sub = lanes(), sublanes()

    if first:
        order = (2, 3, 4, 1, 0, 5, 6, 7)
        copies = {i: pltpu.make_async_copy(far[i], near[i], arrivals.at[i]) for i in order}
        for i in order:
            copies[i].start()
        initial, material, conduct, capacity, substeps, trace_x, trace_y, trace_z = near
        matrix = pairing(False)
        for i in (2, 3, 4, 1):
            copies[i].wait()
        steps = substeps[0]
        prepare(
            steps, matrix, lambda _: copies[0].wait(),
            initial, material, conduct, capacity, cx, cy, cw, cz, weight, scale, start, kcell,
        )
        for source, target in zip(near_links, far_links):
            target[...] = source[...]
        for i in (5, 6, 7):
            copies[i].wait()
        sides = (place_z, 1 - place_z)
        low_tiles, high_tiles = [split([(trace_x, (side, n)) for n in range(NT)], matrix) for side in sides]
        for n in range(NT):
            for j in range(TURN):
                for z in range(2):
                    tile = at_face(n, j, z)
                    face_low[tile, :] = low_tiles(n, j, z)
                    face_high[tile, :] = high_tiles(n, j, z)
                    keep_x[tile, :] = jnp.where(ends_x[0], low_tiles(n, j, z), high_tiles(n, j, z))
        for n in range(NT):
            for x in range(SPAN_X):
                keep_z[n, pl.ds(x, 1), :] = trace_z[n, place_z, pl.ds(x, 1), :]
                come_z[n, pl.ds(x, 1), :] = trace_z[n, 1 - place_z, pl.ds(x, 1), :]
                for side in range(2):
                    spare[pl.ds(SUB * side + SPAN_X * n + x, 1), :] = trace_y[n, x, pl.ds(side, 1), :]
        both = spare[pl.ds(0, 2 * SUB), :]
        both = moved(jnp.concatenate([both, both], 1), matrix)
        for z in range(2):
            spare[pl.ds(2 * SUB * (z + 1), 2 * SUB), :] = both[:, z * SPAN : (z + 1) * SPAN]
        for n in range(NT):
            for i, (x, z) in enumerate(TILES):
                row = SPAN_X * n + x + 2 * SUB * (z + 1)
                keep_y[pl.ds(SUB * n + i, 1), :] = spare[pl.ds(row + SUB * place_y, 1), :]
                come_y[pl.ds(SUB * n + i, 1), :] = spare[pl.ds(row + SUB * (1 - place_y), 1), :]
    else:
        steps = substeps[0]
    last_part = jnp.where(steps == 2, F32(p_robin), F32(2.0 * p_robin))
    mid_part = jnp.where(steps == 2, F32(p_robin), F32(0.0))
    faces_x = ((planes_x[0], face_low, out_high), (planes_x[1], face_high, out_low))

    turned_z[...] = jnp.zeros((SPAN, SPAN), F32)
    inner_z = 1 - place_z
    for n in range(NT):
        for x in range(SPAN_X):
            row = 2 * (SPAN_X * n + x)
            for side, data in ((inner_z, come_z), (place_z, keep_z)):
                line = data[n, pl.ds(x, 1), :]
                place = row + (HALF - 1) * side
                turned_z[pl.ds(place, 1), :] = line
                turned_z[pl.ds((place + HALF) % SPAN, 1), :] = line
    cols_z[...] = turned_z[...].T
    outer_lanes = (lane < HALF // 2) | (lane >= SPAN - HALF // 2)
    low_half = outer_lanes == (lane % 2 == 0)
    for j in range(TURN):
        value = jnp.where(low_half, cols_z[rows_of(j, 0), :], cols_z[rows_of(j, 1), :])
        turned_z[pl.ds(SUB * j, SUB), :] = value
        sum_z[pl.ds(SUB * j, SUB), :] = jnp.zeros((SUB, SPAN), F32)
    for j in range(TURN):
        for p in TILES:
            value = start[at(j, *p), :]
            field[at(j, *p), :] = value
    end_even = (lane == 0) | (lane == HALF)
    end_odd = (lane == HALF - 1) | (lane == SPAN - 1)
    corner_low = (sub == 0) & (lane < HALF)
    corner_high = (sub == SUB - 1) & (lane >= HALF)

    if final:
        back = pairing(True)

    def coarse(n, nothing):
        tile_y = aligned(SUB * n)
        kept, come = keep_y[tile_y, :], come_y[tile_y, :]
        lines[pl.ds(0, SUB), :] = jnp.where(place_y == 0, kept, come)
        lines[pl.ds(SUB, SUB), :] = jnp.where(place_y == 0, come, kept)
        for j in range(TURN):
            column = turned_z[pl.ds(SUB * j, SUB), :]
            for x in range(SPAN_X):
                around = pltpu.roll(column, (SPAN - 2 * x - 2 * SPAN_X * n) % SPAN, 1)
                for z, ends in enumerate((end_even, end_odd)):
                    value = jnp.where(ends, around, 0.0)
                    line = 2 * x + z
                    if j == 0:
                        value = value + jnp.where(corner_low, lines[pl.ds(line, 1), :], 0.0)
                    if j == TURN - 1:
                        value = value + jnp.where(corner_high, lines[pl.ds(SUB + line, 1), :], 0.0)
                    load[at(j, x, z), :] = value * scale[at(j, x, z), :]
        for j in range(TURN):
            for z in range(2):
                tile = at_face(n, j, z)
                for end, (x, data, _) in zip(ends_x, faces_x):
                    value = jnp.where(end, keep_x[tile, :], data[tile, :])
                    at_x_face = aligned(at(j, 0, z).start + 2 * SUB * x)
                    load[at_x_face, :] = load[at_x_face, :] + value * scale[at_x_face, :]

        def substep(index, nothing):
            def to_res(j, here, total):
                for p in TILES:
                    tile = at(j, *p)
                    old[tile, :] = here[p]
                    res[tile, :] = total[p] + weight[tile, :] * here[p] + load[tile, :]

            def to_one(j, here, total):
                for p in TILES:
                    one[at(j, *p), :] = total[p] + here[p]

            def plain(out):
                def emit(j, here, total):
                    for p in TILES:
                        out[at(j, *p), :] = total[p]

                return emit

            def mixed(out, other, factor):
                def emit(j, here, total):
                    for p in TILES:
                        tile = at(j, *p)
                        out[tile, :] = total[p] + factor * other[tile, :]

                return emit

            def close(j, here, total):
                for p in TILES:
                    tile = at(j, *p)
                    field[tile, :] = old[tile, :] + GAIN * (total[p] + QUAD * res[tile, :])

            go = functools.partial(couple, cx, cy, cw, cz)
            go(0, field, to_res)
            go(1, res, to_one)
            go(2, one, plain(two))
            go(3, two, mixed(res, one, SHIFT))
            go(4, res, plain(one))
            go(5, one, mixed(two, res, -RHO2))
            go(6, two, plain(three))
            go(7, three, close)
            return nothing

        lax.fori_loop(0, steps, substep, 0)

        def mean(start_row, last, mid, step=1):
            if step == 1:
                rows = aligned(start_row)
            else:
                rows = pl.ds(start_row, SUB, stride=step)
            return scale[rows, :] * (last * field[rows, :] + mid * old[rows, :])

        planes = []
        for x, data, out in faces_x:
            made = []
            for j in range(TURN):
                pair = []
                for z in range(2):
                    tile = at_face(n, j, z)
                    pair.append(mean(at(j, 0, z).start + 2 * SUB * x, last_part, mid_part) - data[tile, :])
                    if not final:
                        out[tile, :] = pair[z]
                made.append(pair)
            planes.append((out, (n,), made))
        if final:
            join(planes, back)
        for j in range(TURN):
            gathered = sum_z[pl.ds(SUB * j, SUB), :]
            for x in range(SPAN_X):
                value = mean(at(j, x, 0).start + SUB * inner_z, last_part, mid_part)
                shift = 2 * x + 2 * SPAN_X * n
                mine = (lane - (HALF - 1) * inner_z - shift) % HALF == 0
                gathered = gathered + jnp.where(mine, pltpu.roll(value, shift, 1), 0.0)
            sum_z[pl.ds(SUB * j, SUB), :] = gathered
        corner = jnp.where(place_y == 0, at(TURN - 1, 0, 0).start + SUB - 1, 0)
        value = mean(corner, last_part, mid_part, SUB) - come_y[tile_y, :]
        if final:
            value = jnp.where((lane >= HALF) == (place_y == 0), value, other_half(value))
            spare[tile_y, :] = value
        else:
            out_y[tile_y, :] = other_half(value)
        return nothing

    lax.fori_loop(0, NT, coarse, 0)

    for j in range(TURN):
        value = sum_z[pl.ds(SUB * j, SUB), :]
        for half in range(2):
            turned_z[rows_of(j, half), :] = value
    cols_z[...] = turned_z[...].T
    line_lane = lax.broadcasted_iota(jnp.int32, (1, SPAN), 1)
    for n in range(NT):
        for x in range(SPAN_X):
            place = 2 * (SPAN_X * n + x) + (HALF - 1) * inner_z
            low, high = cols_z[pl.ds(place, 1), :], cols_z[pl.ds((place + HALF) % SPAN, 1), :]
            out_z[n, pl.ds(x, 1), :] = jnp.where(line_lane < HALF, low, high) - come_z[n, pl.ds(x, 1), :]
    if final:
        even, odd_z = spare[pl.ds(0, SUB, stride=2), :], spare[pl.ds(1, SUB, stride=2), :]
        both = jnp.concatenate([even, odd_z], 1)
        spare[pl.ds(2 * SUB, 2 * SUB), :] = moved(jnp.concatenate([both, both], 0), back)[:, :SPAN]
        for n in range(NT):
            for x in range(SPAN_X):
                out_y[n, pl.ds(x, 1), :] = spare[pl.ds(2 * SUB + SPAN_X * n + x, 1), :]
        planes = []
        for x in range(SPAN_X):
            made = [[field[at(j, x, z), :] * scale[at(j, x, z), :] for z in range(2)] for j in range(TURN)]
            planes.append((field_out, (x,), made))
        join(planes, back)


def solve(first, final, *operands):
    vmem = pl.BlockSpec(memory_space=pltpu.VMEM)
    smem = pl.BlockSpec(memory_space=pltpu.SMEM)
    far = pl.BlockSpec(memory_space=pltpu.MemorySpace.HBM)
    wide = lambda rows: (rows, SPAN)
    lines_z = (NT, SPAN_X, SPAN)
    if first:
        in_specs = [far] * 8
    else:
        in_specs = [smem] + [vmem] * 14
    shapes = []
    if first:
        shapes += [wide(ROWS_X), wide(ROWS), wide(len(TILES) * SUB)] + [wide(ROWS)] * 4
        shapes += [wide(NT * ROWS_A), wide(NT * SUB), lines_z]
    if final:
        shapes += [(SPAN_X, SPAN, SPAN)]
    shapes += [(NT, SPAN, SPAN) if final else wide(NT * ROWS_A)] * 2
    shapes += [lines_z if final else wide(NT * SUB), lines_z]
    scratch = []
    if first:
        scratch += [pltpu.VMEM(wide(ROWS), F32)] + [pltpu.VMEM(wide(NT * ROWS_A), F32)] * 2
        scratch += [pltpu.VMEM(wide(NT * SUB), F32), pltpu.VMEM(lines_z, F32)]
        for i, operand in enumerate(operands):
            space = pltpu.SMEM if i in (2, 3, 4) else pltpu.VMEM
            scratch.append(space(operand.shape, operand.dtype))
        scratch.append(pltpu.SemaphoreType.DMA((8,)))
    scratch += [pltpu.VMEM(wide(ROWS), F32)] * 7
    scratch += [pltpu.VMEM(wide(ROWS_X), F32)] + [pltpu.VMEM(wide(ROWS), F32)] * 3
    scratch += [pltpu.VMEM(wide(2 * SUB), F32), pltpu.VMEM(wide(6 * SUB), F32)]
    scratch += [pltpu.VMEM(wide(SPAN), F32)] * 2 + [pltpu.VMEM(wide(TURN * SUB), F32)]
    return pl.pallas_call(
        functools.partial(kernel, first, final),
        out_shape=[jax.ShapeDtypeStruct(shape, F32) for shape in shapes],
        in_specs=in_specs,
        out_specs=[vmem] * len(shapes),
        scratch_shapes=scratch,
        compiler_params=pltpu.CompilerParams(vmem_limit_bytes=24 * 1024 * 1024),
    )(*operands)


def exchange(out_low, out_high, out_y, out_z):
    count = lax.axis_size("gx")
    cores = lax.axis_size("gz")

    def turn(way):
        pairs = []
        for i in range(count):
            for z in range(cores):
                to = i + (way if z == 0 else -way)
                pairs.append((i * cores + z, to * cores + z if 0 <= to < count else i * cores + 1 - z))
        return pairs

    swap = [(0, 1), (1, 0)]
    return (
        lax.ppermute(out_low, ("gx", "gz"), turn(1)),
        lax.ppermute(out_high, ("gx", "gz"), turn(-1)),
        lax.ppermute(out_y, "gy", swap),
        lax.ppermute(out_z, "gz", swap),
    )


def local(initial, material, conduct, capacity, substeps, trace_x, trace_y, trace_z):
    steps = substeps.reshape(1)
    place_x, place_y, place_z = (lax.axis_index("gx"), lax.axis_index("gy"), lax.axis_index("gz"))
    inputs = (initial, material, conduct, capacity, steps, trace_x, trace_y, trace_z)
    hold = lambda value: pltpu.with_memory_space_constraint(value, pltpu.MemorySpace.HBM)
    inputs = [value if value is steps else hold(value) for value in inputs]
    results = solve(True, False, *inputs)
    prepared, sent = results[:10], results[10:]
    for iteration in range(1, ITERS):
        arrived = exchange(*sent)
        final = iteration == ITERS - 1
        sent = solve(False, final, steps, *prepared, *arrived)
    field, *sent = sent
    face_low, face_high, come_y, come_z = exchange(*sent)
    face_low, face_high = (
        jnp.where(place_z == 0, face_low, face_high),
        jnp.where(place_z == 0, face_high, face_low),
    )
    face_low = jnp.where(place_x == 0, trace_x[0], face_low)
    face_high = jnp.where(place_x == lax.axis_size("gx") - 1, trace_x[1], face_high)
    got_x = jnp.stack([face_low, face_high], 0)
    got_y = jnp.stack([jnp.where(place_y == side, trace_y[:, :, side], come_y) for side in range(2)], 2)
    got_z = jnp.stack([jnp.where(place_z == side, trace_z[:, side], come_z) for side in range(2)], 1)
    return (field, got_x, got_y, got_z)


def solution(mesh):
    placed = (
        P("gx", "gy", "gz"),
        P("gx", "gy", "gz"),
        P(),
        P(),
        P("gx", "gy", "gz"),
        P("gx", None, "gy", "gz"),
        P(None, "gx", "gy", "gz"),
        P(None, "gz", "gx", "gy"),
    )
    return jax.shard_map(
        local,
        mesh=mesh,
        in_specs=placed,
        out_specs=(
            P("gx", "gy", "gz"),
            P("gx", None, "gy", "gz"),
            P(None, "gx", "gy", "gz"),
            P(None, "gz", "gx", "gy"),
        ),
        check_vma=False,
    )
```

```python
import functools

import jax
import jax.numpy as jnp
from jax import lax
from jax.experimental import pallas as pl
from jax.experimental.pallas import tpu as pltpu
from jax.sharding import PartitionSpec as P

NT = 2
SWEEPS = 8
ITERS = 4
NMAT = 8
SPAN_X = 4
SPAN = 128
HALF = SPAN // 2
SUB = 8
TURN = 8

p_robin = 1.5
dt_coarse = 0.5
rho_bound = 0.9

RHO2 = rho_bound**2
SHIFT = 1.0 - RHO2
QUAD = RHO2 * RHO2 / 4.0 + SHIFT
Y_ONE = 2.0 / RHO2 - 1.0
GAIN = 128.0 / (RHO2**4 * (8.0 * Y_ONE**4 - 8.0 * Y_ONE**2 + 1.0))

F32 = jnp.float32
TILES = [(x, z) for x in range(SPAN_X) for z in range(2)]
ROWS = TURN * len(TILES) * SUB
ROWS_X = TURN * (SPAN_X - 1) * 2 * SUB
ROWS_A = TURN * 2 * SUB


def at(j, x, z):
    return pl.ds(((j * SPAN_X + x) * 2 + z) * SUB, SUB)


def at_x(j, x, z):
    return pl.ds(((j * (SPAN_X - 1) + x) * 2 + z) * SUB, SUB)


def at_face(n, j, z):
    return pl.ds(pl.multiple_of(((n * TURN + j) * 2 + z) * SUB, SUB), SUB)


def aligned(rows):
    return pl.ds(pl.multiple_of(rows, SUB), SUB)


def lanes():
    return lax.broadcasted_iota(jnp.int32, (SUB, SPAN), 1)


def sublanes():
    return lax.broadcasted_iota(jnp.int32, (SUB, SPAN), 0)


def harmonic(left_k, right_k):
    return 2.0 * left_k * right_k / (left_k + right_k)


def pick(bits, table_ref):
    level = [table_ref[i] for i in range(NMAT)]
    for bit in bits:
        level = [jnp.where(bit, level[2 * i + 1], level[2 * i]) for i in range(len(level) // 2)]
    return level[0]


def up_z(value):
    return pltpu.roll(value, SPAN - 1, 1)


def down_z(value):
    return pltpu.roll(value, 1, 1)


def other_half(value):
    return pltpu.roll(value, HALF, 1)


def up_y(value):
    turned = pltpu.roll(value, SUB - 1, 0)
    return jnp.where(sublanes() < SUB - 1, turned, other_half(turned))


def down_y(value):
    turned = pltpu.roll(value, 1, 0)
    return jnp.where(sublanes() > 0, turned, other_half(turned))


def pairing(back):
    row = lax.broadcasted_iota(jnp.int32, (2 * SPAN, 2 * SPAN), 1 if back else 0)
    col = lax.broadcasted_iota(jnp.int32, (2 * SPAN, 2 * SPAN), 0 if back else 1)
    half, z = row // SPAN, row % SPAN
    place = (z % 2) * SPAN + half * HALF + z // 2
    return jnp.where(col == place, 1.0, 0.0).astype(jnp.bfloat16)


def moved(value, matrix, narrow=False):
    dot = functools.partial(jnp.dot, preferred_element_type=F32)
    high = value.astype(jnp.bfloat16)
    if narrow:
        return dot(high, matrix)
    rest = value - high.astype(F32)
    middle = rest.astype(jnp.bfloat16)
    low = (rest - middle.astype(F32)).astype(jnp.bfloat16)
    return dot(high, matrix) + (dot(middle, matrix) + dot(low, matrix))


def rows_of(j, half):
    return pl.ds(HALF * half + j, SUB, stride=TURN)


def split(planes, matrix, narrow=False):
    pieces = []
    for ref, lead in planes:
        for j in range(TURN):
            halves = [ref[(*lead, rows_of(j, half), slice(None))].astype(F32) for half in range(2)]
            pieces.append(jnp.concatenate(halves, 1))
    out = moved(jnp.concatenate(pieces, 0), matrix, narrow)

    def tile(plane, j, z):
        row = (plane * TURN + j) * SUB
        return out[row : row + SUB, z * SPAN : (z + 1) * SPAN]

    return tile


def join(planes, matrix):
    pieces = [jnp.concatenate(tiles[j], 1) for _, _, tiles in planes for j in range(TURN)]
    out = moved(jnp.concatenate(pieces, 0), matrix)
    for plane, (ref, lead, _) in enumerate(planes):
        for j in range(TURN):
            row = (plane * TURN + j) * SUB
            for half in range(2):
                ref[(*lead, rows_of(j, half), slice(None))] = out[row : row + SUB, half * SPAN : (half + 1) * SPAN]


def prepare(steps, matrix, arrive, initial, material, conduct, capacity, cx, cy, cw, cz, weight, scale, start, kcell):
    lane, sub = lanes(), sublanes()
    inverse_h = steps.astype(F32) * (1.0 / dt_coarse)
    tiles = split([(material, (x,)) for x in range(SPAN_X)], matrix, narrow=True)
    for j in range(TURN):
        for x in range(SPAN_X):
            for z in range(2):
                mat = tiles(x, j, z).astype(jnp.int32)
                bits = [(mat & 1) != 0, (mat & 2) != 0, (mat & 4) != 0]
                kcell[at(j, x, z), :] = pick(bits, conduct)
                start[at(j, x, z), :] = pick(bits, capacity)
    inner = (lane != HALF - 1) & (lane != SPAN - 1)
    for j in range(TURN):
        for x, z in TILES:
            here = kcell[at(j, x, z), :]
            if x < SPAN_X - 1:
                cx[at_x(j, x, z), :] = harmonic(here, kcell[at(j, x + 1, z), :])
            if j < TURN - 1:
                cy[at(j, x, z), :] = harmonic(here, kcell[at(j + 1, x, z), :])
            else:
                link = harmonic(here, up_y(kcell[at(0, x, z), :]))
                cy[at(j, x, z), :] = jnp.where((sub == SUB - 1) & (lane >= HALF), 0.0, link)
            if z == 0:
                cz[at(j, x, z), :] = harmonic(here, kcell[at(j, x, 1), :])
            else:
                cz[at(j, x, z), :] = jnp.where(inner, harmonic(here, up_z(kcell[at(j, x, 0), :])), 0.0)
    for j in range(TURN):
        for x, z in TILES:
            base = cz[at(j, x, 0), :] + (cz[at(j, x, 1), :] if z else down_z(cz[at(j, x, 1), :]))
            base = base + cy[at(j, x, z), :]
            base = base + (cy[at(j - 1, x, z), :] if j > 0 else down_y(cy[at(TURN - 1, x, z), :]))
            if x < SPAN_X - 1:
                base = base + cx[at_x(j, x, z), :]
            if x > 0:
                base = base + cx[at_x(j, x - 1, z), :]
            if x in (0, SPAN_X - 1):
                base = base + p_robin
            end = HALF - 1 if z else 0
            base = base + jnp.where((lane == end) | (lane == end + HALF), p_robin, 0.0)
            if j == 0:
                base = base + jnp.where((sub == 0) & (lane < HALF), p_robin, 0.0)
            if j == TURN - 1:
                base = base + jnp.where((sub == SUB - 1) & (lane >= HALF), p_robin, 0.0)
            diagonal = start[at(j, x, z), :] * inverse_h + base
            root = lax.rsqrt(diagonal)
            root = root * (1.5 - 0.5 * diagonal * root * root)
            scale[at(j, x, z), :] = root
            weight[at(j, x, z), :] = -base * root * root
            start[at(j, x, z), :] = diagonal * root
    for j in range(TURN):
        for x, z in TILES:
            here = scale[at(j, x, z), :]
            if x < SPAN_X - 1:
                cx[at_x(j, x, z), :] = cx[at_x(j, x, z), :] * here * scale[at(j, x + 1, z), :]
            after = scale[at(j + 1, x, z), :] if j < TURN - 1 else up_y(scale[at(0, x, z), :])
            cy[at(j, x, z), :] = cy[at(j, x, z), :] * here * after
            beside = up_z(scale[at(j, x, 0), :]) if z else scale[at(j, x, 1), :]
            cz[at(j, x, z), :] = cz[at(j, x, z), :] * here * beside
    for x, z in TILES:
        cw[at(0, x, z), :] = down_y(cy[at(TURN - 1, x, z), :])
    arrive(1)
    tiles = split([(initial, (x,)) for x in range(SPAN_X)], matrix)
    for j in range(TURN):
        for x, z in TILES:
            start[at(j, x, z), :] = start[at(j, x, z), :] * tiles(x, j, z)


def couple(cx, cy, cw, cz, begin, source, emit):
    def load(j):
        return {p: source[at(j, *p), :] for p in TILES}

    def wrap_down(row):
        return {p: cw[at(0, *p), :] * down_y(row[p]) for p in TILES}

    here = load(begin)
    before = load((begin - 1) % TURN)
    if begin == 0:
        before = wrap_down(before)
    else:
        before = {p: cy[at(begin - 1, *p), :] * before[p] for p in TILES}
    for turn in range(TURN):
        j = (begin + turn) % TURN
        following = load((j + 1) % TURN)
        after = following if j < TURN - 1 else {p: up_y(following[p]) for p in TILES}
        total, later = {}, {}
        for p in TILES:
            link = cy[at(j, *p), :]
            total[p] = before[p] + link * after[p]
            if j < TURN - 1:
                later[p] = link * here[p]
        for x in range(SPAN_X):
            even, odd = (x, 0), (x, 1)
            link = cz[at(j, *even), :]
            total[even] = total[even] + link * here[odd]
            total[odd] = total[odd] + link * here[even]
            link = cz[at(j, *odd), :]
            total[odd] = total[odd] + link * up_z(here[even])
            total[even] = total[even] + down_z(link * here[odd])
        for x in range(SPAN_X - 1):
            for z in range(2):
                link = cx[at_x(j, x, z), :]
                total[(x, z)] = total[(x, z)] + link * here[(x + 1, z)]
                total[(x + 1, z)] = total[(x + 1, z)] + link * here[(x, z)]
        emit(j, here, total)
        before = later if j < TURN - 1 else wrap_down(here)
        here = following


def kernel(first, final, *refs):
    refs = list(refs)
    take = lambda n: [refs.pop(0) for _ in range(n)]
    if first:
        far = take(8)
        outer_y, cx, cy, cw, cz, weight, scale, start, keep_x, keep_y, keep_z = take(11)
    else:
        (substeps,) = take(1)
        cx, cy, cw, cz, weight, scale, start, keep_x, keep_y, keep_z = take(10)
        face_low, face_high, come_y, come_z = take(4)
    if final:
        (field_out,) = take(1)
    out_low, out_high, out_y, out_z = take(4)
    if first:
        kcell, face_low, face_high, come_y, come_z = take(5)
        near = take(8)
        (arrivals,) = take(1)
    field, old, load, res, one, two, three = take(7)
    near_links, far_links = take(4), (cx, cy, cz, weight)
    if not first:
        for source, target in zip(far_links, near_links):
            target[...] = source[...]
    cx, cy, cz, weight = near_links
    lines, spare, turned_z, cols_z, sum_z = take(5)

    place_x, place_y, place_z = (lax.axis_index("gx"), lax.axis_index("gy"), lax.axis_index("gz"))
    planes_x = ((SPAN_X - 1) * place_z, (SPAN_X - 1) * (1 - place_z))
    outer_x = [jnp.where(plane == 0, 0, lax.axis_size("gx") - 1) for plane in planes_x]
    ends_x = [place_x == outer for outer in outer_x]
    lane, sub = lanes(), sublanes()

    if first:
        order = (2, 3, 4, 1, 0, 5, 6, 7)
        copies = {i: pltpu.make_async_copy(far[i], near[i], arrivals.at[i]) for i in order}
        for i in order:
            copies[i].start()
        initial, material, conduct, capacity, substeps, trace_x, trace_y, trace_z = near
        matrix = pairing(False)
        for i in (2, 3, 4, 1):
            copies[i].wait()
        steps = substeps[0]
        prepare(
            steps, matrix, lambda _: copies[0].wait(),
            initial, material, conduct, capacity, cx, cy, cw, cz, weight, scale, start, kcell,
        )
        for source, target in zip(near_links, far_links):
            target[...] = source[...]
        for i in (5, 6, 7):
            copies[i].wait()
        sides = (place_z, 1 - place_z)
        low_tiles, high_tiles = [split([(trace_x, (side, n)) for n in range(NT)], matrix) for side in sides]
        for n in range(NT):
            for j in range(TURN):
                for z in range(2):
                    tile = at_face(n, j, z)
                    face_low[tile, :] = low_tiles(n, j, z)
                    face_high[tile, :] = high_tiles(n, j, z)
                    keep_x[tile, :] = jnp.where(ends_x[0], low_tiles(n, j, z), high_tiles(n, j, z))
        for n in range(NT):
            for x in range(SPAN_X):
                keep_z[n, pl.ds(x, 1), :] = trace_z[n, place_z, pl.ds(x, 1), :]
                come_z[n, pl.ds(x, 1), :] = trace_z[n, 1 - place_z, pl.ds(x, 1), :]
                outer_y[n, pl.ds(x, 1), :] = trace_y[n, x, pl.ds(place_y, 1), :]
                for side in range(2):
                    spare[pl.ds(SUB * side + SPAN_X * n + x, 1), :] = trace_y[n, x, pl.ds(side, 1), :]
        both = spare[pl.ds(0, 2 * SUB), :]
        both = moved(jnp.concatenate([both, both], 1), matrix)
        for z in range(2):
            spare[pl.ds(2 * SUB * (z + 1), 2 * SUB), :] = both[:, z * SPAN : (z + 1) * SPAN]
        for n in range(NT):
            for i, (x, z) in enumerate(TILES):
                row = SPAN_X * n + x + 2 * SUB * (z + 1)
                keep_y[pl.ds(SUB * n + i, 1), :] = spare[pl.ds(row + SUB * place_y, 1), :]
                come_y[pl.ds(SUB * n + i, 1), :] = spare[pl.ds(row + SUB * (1 - place_y), 1), :]
    else:
        steps = substeps[0]
    last_part = jnp.where(steps == 2, F32(p_robin), F32(2.0 * p_robin))
    mid_part = jnp.where(steps == 2, F32(p_robin), F32(0.0))
    faces_x = ((planes_x[0], face_low, out_high), (planes_x[1], face_high, out_low))

    turned_z[...] = jnp.zeros((SPAN, SPAN), F32)
    inner_z = 1 - place_z
    for n in range(NT):
        for x in range(SPAN_X):
            row = 2 * (SPAN_X * n + x)
            for side, data in ((inner_z, come_z), (place_z, keep_z)):
                line = data[n, pl.ds(x, 1), :]
                place = row + (HALF - 1) * side
                turned_z[pl.ds(place, 1), :] = line
                turned_z[pl.ds((place + HALF) % SPAN, 1), :] = line
    cols_z[...] = turned_z[...].T
    outer_lanes = (lane < HALF // 2) | (lane >= SPAN - HALF // 2)
    low_half = outer_lanes == (lane % 2 == 0)
    for j in range(TURN):
        value = jnp.where(low_half, cols_z[rows_of(j, 0), :], cols_z[rows_of(j, 1), :])
        turned_z[pl.ds(SUB * j, SUB), :] = value
        sum_z[pl.ds(SUB * j, SUB), :] = jnp.zeros((SUB, SPAN), F32)
    for j in range(TURN):
        for p in TILES:
            value = start[at(j, *p), :]
            field[at(j, *p), :] = value
    end_even = (lane == 0) | (lane == HALF)
    end_odd = (lane == HALF - 1) | (lane == SPAN - 1)
    corner_low = (sub == 0) & (lane < HALF)
    corner_high = (sub == SUB - 1) & (lane >= HALF)

    if final:
        back = pairing(True)

    def coarse(n, nothing):
        tile_y = aligned(SUB * n)
        kept, come = keep_y[tile_y, :], come_y[tile_y, :]
        lines[pl.ds(0, SUB), :] = jnp.where(place_y == 0, kept, come)
        lines[pl.ds(SUB, SUB), :] = jnp.where(place_y == 0, come, kept)
        for j in range(TURN):
            column = turned_z[pl.ds(SUB * j, SUB), :]
            for x in range(SPAN_X):
                around = pltpu.roll(column, (SPAN - 2 * x - 2 * SPAN_X * n) % SPAN, 1)
                for z, ends in enumerate((end_even, end_odd)):
                    value = jnp.where(ends, around, 0.0)
                    line = 2 * x + z
                    if j == 0:
                        value = value + jnp.where(corner_low, lines[pl.ds(line, 1), :], 0.0)
                    if j == TURN - 1:
                        value = value + jnp.where(corner_high, lines[pl.ds(SUB + line, 1), :], 0.0)
                    load[at(j, x, z), :] = value * scale[at(j, x, z), :]
        for j in range(TURN):
            for z in range(2):
                tile = at_face(n, j, z)
                for end, (x, data, _) in zip(ends_x, faces_x):
                    value = jnp.where(end, keep_x[tile, :], data[tile, :])
                    at_x_face = aligned(at(j, 0, z).start + 2 * SUB * x)
                    load[at_x_face, :] = load[at_x_face, :] + value * scale[at_x_face, :]

        def substep(index, nothing):
            def to_res(j, here, total):
                for p in TILES:
                    tile = at(j, *p)
                    old[tile, :] = here[p]
                    res[tile, :] = total[p] + weight[tile, :] * here[p] + load[tile, :]

            def to_one(j, here, total):
                for p in TILES:
                    one[at(j, *p), :] = total[p] + here[p]

            def plain(out):
                def emit(j, here, total):
                    for p in TILES:
                        out[at(j, *p), :] = total[p]

                return emit

            def mixed(out, other, factor):
                def emit(j, here, total):
                    for p in TILES:
                        tile = at(j, *p)
                        out[tile, :] = total[p] + factor * other[tile, :]

                return emit

            def close(j, here, total):
                for p in TILES:
                    tile = at(j, *p)
                    field[tile, :] = old[tile, :] + GAIN * (total[p] + QUAD * res[tile, :])

            go = functools.partial(couple, cx, cy, cw, cz)
            go(0, field, to_res)
            go(1, res, to_one)
            go(2, one, plain(two))
            go(3, two, mixed(res, one, SHIFT))
            go(4, res, plain(one))
            go(5, one, mixed(two, res, -RHO2))
            go(6, two, plain(three))
            go(7, three, close)
            return nothing

        lax.fori_loop(0, steps, substep, 0)

        def mean(start_row, last, mid, step=1):
            if step == 1:
                rows = aligned(start_row)
            else:
                rows = pl.ds(start_row, SUB, stride=step)
            return scale[rows, :] * (last * field[rows, :] + mid * old[rows, :])

        planes = []
        for x, data, out in faces_x:
            made = []
            for j in range(TURN):
                pair = []
                for z in range(2):
                    tile = at_face(n, j, z)
                    pair.append(mean(at(j, 0, z).start + 2 * SUB * x, last_part, mid_part) - data[tile, :])
                    if not final:
                        out[tile, :] = pair[z]
                made.append(pair)
            planes.append((out, (n,), made))
        if final:
            join(planes, back)
        for j in range(TURN):
            gathered = sum_z[pl.ds(SUB * j, SUB), :]
            for x in range(SPAN_X):
                value = mean(at(j, x, 0).start + SUB * inner_z, last_part, mid_part)
                shift = 2 * x + 2 * SPAN_X * n
                mine = (lane - (HALF - 1) * inner_z - shift) % HALF == 0
                gathered = gathered + jnp.where(mine, pltpu.roll(value, shift, 1), 0.0)
            sum_z[pl.ds(SUB * j, SUB), :] = gathered
        corner = jnp.where(place_y == 0, at(TURN - 1, 0, 0).start + SUB - 1, 0)
        value = mean(corner, last_part, mid_part, SUB) - come_y[tile_y, :]
        if final:
            value = jnp.where((lane >= HALF) == (place_y == 0), value, other_half(value))
            spare[tile_y, :] = value
        else:
            out_y[tile_y, :] = other_half(value)
        return nothing

    lax.fori_loop(0, NT, coarse, 0)

    for j in range(TURN):
        value = sum_z[pl.ds(SUB * j, SUB), :]
        for half in range(2):
            turned_z[rows_of(j, half), :] = value
    cols_z[...] = turned_z[...].T
    line_lane = lax.broadcasted_iota(jnp.int32, (1, SPAN), 1)
    for n in range(NT):
        for x in range(SPAN_X):
            place = 2 * (SPAN_X * n + x) + (HALF - 1) * inner_z
            low, high = cols_z[pl.ds(place, 1), :], cols_z[pl.ds((place + HALF) % SPAN, 1), :]
            out_z[n, pl.ds(x, 1), :] = jnp.where(line_lane < HALF, low, high) - come_z[n, pl.ds(x, 1), :]
    if final:
        even, odd_z = spare[pl.ds(0, SUB, stride=2), :], spare[pl.ds(1, SUB, stride=2), :]
        both = jnp.concatenate([even, odd_z], 1)
        spare[pl.ds(2 * SUB, 2 * SUB), :] = moved(jnp.concatenate([both, both], 0), back)[:, :SPAN]
        for n in range(NT):
            for x in range(SPAN_X):
                out_y[n, pl.ds(x, 1), :] = spare[pl.ds(2 * SUB + SPAN_X * n + x, 1), :]
        field_out[...] = field[...] * scale[...]


def solve(first, final, *operands):
    vmem = pl.BlockSpec(memory_space=pltpu.VMEM)
    smem = pl.BlockSpec(memory_space=pltpu.SMEM)
    far = pl.BlockSpec(memory_space=pltpu.MemorySpace.HBM)
    wide = lambda rows: (rows, SPAN)
    lines_z = (NT, SPAN_X, SPAN)
    if first:
        in_specs = [far] * 8
    else:
        in_specs = [smem] + [vmem] * 14
    shapes = []
    if first:
        shapes += [lines_z, wide(ROWS_X), wide(ROWS), wide(len(TILES) * SUB)] + [wide(ROWS)] * 4
        shapes += [wide(NT * ROWS_A), wide(NT * SUB), lines_z]
    if final:
        shapes += [wide(ROWS)]
    shapes += [(NT, SPAN, SPAN) if final else wide(NT * ROWS_A)] * 2
    shapes += [lines_z if final else wide(NT * SUB), lines_z]
    scratch = []
    if first:
        scratch += [pltpu.VMEM(wide(ROWS), F32)] + [pltpu.VMEM(wide(NT * ROWS_A), F32)] * 2
        scratch += [pltpu.VMEM(wide(NT * SUB), F32), pltpu.VMEM(lines_z, F32)]
        for i, operand in enumerate(operands):
            space = pltpu.SMEM if i in (2, 3, 4) else pltpu.VMEM
            scratch.append(space(operand.shape, operand.dtype))
        scratch.append(pltpu.SemaphoreType.DMA((8,)))
    scratch += [pltpu.VMEM(wide(ROWS), F32)] * 7
    scratch += [pltpu.VMEM(wide(ROWS_X), F32)] + [pltpu.VMEM(wide(ROWS), F32)] * 3
    scratch += [pltpu.VMEM(wide(2 * SUB), F32), pltpu.VMEM(wide(6 * SUB), F32)]
    scratch += [pltpu.VMEM(wide(SPAN), F32)] * 2 + [pltpu.VMEM(wide(TURN * SUB), F32)]
    return pl.pallas_call(
        functools.partial(kernel, first, final),
        out_shape=[jax.ShapeDtypeStruct(shape, F32) for shape in shapes],
        in_specs=in_specs,
        out_specs=[vmem] * len(shapes),
        scratch_shapes=scratch,
        compiler_params=pltpu.CompilerParams(vmem_limit_bytes=24 * 1024 * 1024),
    )(*operands)


def unfold(field, out):
    planes = []
    for x in range(SPAN_X):
        made = [[field[at(j, x, z), :] for z in range(2)] for j in range(TURN)]
        planes.append((out, (x,), made))
    join(planes, pairing(True))


def exchange(out_low, out_high, out_y, out_z):
    count = lax.axis_size("gx")
    cores = lax.axis_size("gz")

    def turn(way):
        pairs = []
        for i in range(count):
            for z in range(cores):
                to = i + (way if z == 0 else -way)
                pairs.append((i * cores + z, to * cores + z if 0 <= to < count else i * cores + 1 - z))
        return pairs

    swap = [(0, 1), (1, 0)]
    return (
        lax.ppermute(out_low, ("gx", "gz"), turn(1)),
        lax.ppermute(out_high, ("gx", "gz"), turn(-1)),
        lax.ppermute(out_y, "gy", swap),
        lax.ppermute(out_z, "gz", swap),
    )


def local(initial, material, conduct, capacity, substeps, trace_x, trace_y, trace_z):
    steps = substeps.reshape(1)
    place_x, place_y, place_z = (lax.axis_index("gx"), lax.axis_index("gy"), lax.axis_index("gz"))
    inputs = (initial, material, conduct, capacity, steps, trace_x, trace_y, trace_z)
    hold = lambda value: pltpu.with_memory_space_constraint(value, pltpu.MemorySpace.HBM)
    inputs = [value if value is steps else hold(value) for value in inputs]
    results = solve(True, False, *inputs)
    outer_y, *prepared = results[:11]
    outer_z, sent = prepared[-1], results[11:]
    for iteration in range(1, ITERS):
        arrived = exchange(*sent)
        final = iteration == ITERS - 1
        sent = solve(False, final, steps, *prepared, *arrived)
    field, *sent = sent
    face_low, face_high, come_y, come_z = exchange(*sent)
    face_low, face_high = (
        jnp.where(place_z == 0, face_low, face_high),
        jnp.where(place_z == 0, face_high, face_low),
    )
    face_low = jnp.where(place_x == 0, trace_x[0], face_low)
    face_high = jnp.where(place_x == lax.axis_size("gx") - 1, trace_x[1], face_high)
    got_x = jnp.stack([face_low, face_high], 0)
    got_y = jnp.stack([jnp.where(place_y == side, outer_y, come_y) for side in range(2)], 2)
    got_z = jnp.stack([jnp.where(place_z == side, outer_z, come_z) for side in range(2)], 1)
    vmem = pl.BlockSpec(memory_space=pltpu.VMEM)
    thermal = pl.pallas_call(
        unfold,
        out_shape=jax.ShapeDtypeStruct((SPAN_X, SPAN, SPAN), F32),
        in_specs=[vmem],
        out_specs=vmem,
        cost_estimate=pl.CostEstimate(flops=10**8, bytes_accessed=10**6, transcendentals=0),
    )(pltpu.with_memory_space_constraint(field, pltpu.MemorySpace.VMEM))
    return (thermal, got_x, got_y, got_z)


def solution(mesh):
    placed = (
        P("gx", "gy", "gz"),
        P("gx", "gy", "gz"),
        P(),
        P(),
        P("gx", "gy", "gz"),
        P("gx", None, "gy", "gz"),
        P(None, "gx", "gy", "gz"),
        P(None, "gz", "gx", "gy"),
    )
    return jax.shard_map(
        local,
        mesh=mesh,
        in_specs=placed,
        out_specs=(
            P("gx", "gy", "gz"),
            P("gx", None, "gy", "gz"),
            P(None, "gx", "gy", "gz"),
            P(None, "gz", "gx", "gy"),
        ),
        check_vma=False,
    )
```

```python
import functools

import jax
import jax.numpy as jnp
from jax import lax
from jax.experimental import pallas as pl
from jax.experimental.pallas import tpu as pltpu
from jax.sharding import PartitionSpec as P

NT = 2
SWEEPS = 8
ITERS = 4
NMAT = 8
SPAN_X = 4
SPAN = 128
HALF = SPAN // 2
SUB = 8
TURN = 8

p_robin = 1.5
dt_coarse = 0.5
rho_bound = 0.9

RHO2 = rho_bound**2
SHIFT = 1.0 - RHO2
QUAD = RHO2 * RHO2 / 4.0 + SHIFT
Y_ONE = 2.0 / RHO2 - 1.0
GAIN = 128.0 / (RHO2**4 * (8.0 * Y_ONE**4 - 8.0 * Y_ONE**2 + 1.0))

F32 = jnp.float32
TILES = [(x, z) for x in range(SPAN_X) for z in range(2)]
ROWS = TURN * len(TILES) * SUB
ROWS_X = TURN * (SPAN_X - 1) * 2 * SUB
ROWS_A = TURN * 2 * SUB


def at(j, x, z):
    return pl.ds(((j * SPAN_X + x) * 2 + z) * SUB, SUB)


def at_x(j, x, z):
    return pl.ds(((j * (SPAN_X - 1) + x) * 2 + z) * SUB, SUB)


def at_face(n, j, z):
    return pl.ds(pl.multiple_of(((n * TURN + j) * 2 + z) * SUB, SUB), SUB)


def aligned(rows):
    return pl.ds(pl.multiple_of(rows, SUB), SUB)


def lanes():
    return lax.broadcasted_iota(jnp.int32, (SUB, SPAN), 1)


def sublanes():
    return lax.broadcasted_iota(jnp.int32, (SUB, SPAN), 0)


def harmonic(left_k, right_k):
    return 2.0 * left_k * right_k / (left_k + right_k)


def pick(bits, table_ref):
    level = [table_ref[i] for i in range(NMAT)]
    for bit in bits:
        level = [jnp.where(bit, level[2 * i + 1], level[2 * i]) for i in range(len(level) // 2)]
    return level[0]


def up_z(value):
    return pltpu.roll(value, SPAN - 1, 1)


def down_z(value):
    return pltpu.roll(value, 1, 1)


def other_half(value):
    return pltpu.roll(value, HALF, 1)


def up_y(value):
    turned = pltpu.roll(value, SUB - 1, 0)
    return jnp.where(sublanes() < SUB - 1, turned, other_half(turned))


def down_y(value):
    turned = pltpu.roll(value, 1, 0)
    return jnp.where(sublanes() > 0, turned, other_half(turned))


def pairing(back):
    row = lax.broadcasted_iota(jnp.int32, (2 * SPAN, 2 * SPAN), 1 if back else 0)
    col = lax.broadcasted_iota(jnp.int32, (2 * SPAN, 2 * SPAN), 0 if back else 1)
    half, z = row // SPAN, row % SPAN
    place = (z % 2) * SPAN + half * HALF + z // 2
    return jnp.where(col == place, 1.0, 0.0).astype(jnp.bfloat16)


def moved(value, matrix, narrow=False):
    dot = functools.partial(jnp.dot, preferred_element_type=F32)
    high = value.astype(jnp.bfloat16)
    if narrow:
        return dot(high, matrix)
    rest = value - high.astype(F32)
    middle = rest.astype(jnp.bfloat16)
    low = (rest - middle.astype(F32)).astype(jnp.bfloat16)
    return dot(high, matrix) + (dot(middle, matrix) + dot(low, matrix))


def rows_of(j, half):
    return pl.ds(HALF * half + j, SUB, stride=TURN)


def split(planes, matrix, narrow=False):
    pieces = []
    for ref, lead in planes:
        for j in range(TURN):
            halves = [ref[(*lead, rows_of(j, half), slice(None))].astype(F32) for half in range(2)]
            pieces.append(jnp.concatenate(halves, 1))
    out = moved(jnp.concatenate(pieces, 0), matrix, narrow)

    def tile(plane, j, z):
        row = (plane * TURN + j) * SUB
        return out[row : row + SUB, z * SPAN : (z + 1) * SPAN]

    return tile


def join(planes, matrix):
    pieces = [jnp.concatenate(tiles[j], 1) for _, _, tiles in planes for j in range(TURN)]
    out = moved(jnp.concatenate(pieces, 0), matrix)
    for plane, (ref, lead, _) in enumerate(planes):
        for j in range(TURN):
            row = (plane * TURN + j) * SUB
            for half in range(2):
                ref[(*lead, rows_of(j, half), slice(None))] = out[row : row + SUB, half * SPAN : (half + 1) * SPAN]


def prepare(steps, matrix, arrive, initial, material, conduct, capacity, cx, cy, cw, cz, weight, scale, start, kcell):
    lane, sub = lanes(), sublanes()
    inverse_h = steps.astype(F32) * (1.0 / dt_coarse)
    tiles = split([(material, (x,)) for x in range(SPAN_X)], matrix, narrow=True)
    for j in range(TURN):
        for x in range(SPAN_X):
            for z in range(2):
                mat = tiles(x, j, z).astype(jnp.int32)
                bits = [(mat & 1) != 0, (mat & 2) != 0, (mat & 4) != 0]
                kcell[at(j, x, z), :] = pick(bits, conduct)
                start[at(j, x, z), :] = pick(bits, capacity)
    inner = (lane != HALF - 1) & (lane != SPAN - 1)
    for j in range(TURN):
        for x, z in TILES:
            here = kcell[at(j, x, z), :]
            if x < SPAN_X - 1:
                cx[at_x(j, x, z), :] = harmonic(here, kcell[at(j, x + 1, z), :])
            if j < TURN - 1:
                cy[at(j, x, z), :] = harmonic(here, kcell[at(j + 1, x, z), :])
            else:
                link = harmonic(here, up_y(kcell[at(0, x, z), :]))
                cy[at(j, x, z), :] = jnp.where((sub == SUB - 1) & (lane >= HALF), 0.0, link)
            if z == 0:
                cz[at(j, x, z), :] = harmonic(here, kcell[at(j, x, 1), :])
            else:
                cz[at(j, x, z), :] = jnp.where(inner, harmonic(here, up_z(kcell[at(j, x, 0), :])), 0.0)
    for j in range(TURN):
        for x, z in TILES:
            base = cz[at(j, x, 0), :] + (cz[at(j, x, 1), :] if z else down_z(cz[at(j, x, 1), :]))
            base = base + cy[at(j, x, z), :]
            base = base + (cy[at(j - 1, x, z), :] if j > 0 else down_y(cy[at(TURN - 1, x, z), :]))
            if x < SPAN_X - 1:
                base = base + cx[at_x(j, x, z), :]
            if x > 0:
                base = base + cx[at_x(j, x - 1, z), :]
            if x in (0, SPAN_X - 1):
                base = base + p_robin
            end = HALF - 1 if z else 0
            base = base + jnp.where((lane == end) | (lane == end + HALF), p_robin, 0.0)
            if j == 0:
                base = base + jnp.where((sub == 0) & (lane < HALF), p_robin, 0.0)
            if j == TURN - 1:
                base = base + jnp.where((sub == SUB - 1) & (lane >= HALF), p_robin, 0.0)
            diagonal = start[at(j, x, z), :] * inverse_h + base
            root = lax.rsqrt(diagonal)
            root = root * (1.5 - 0.5 * diagonal * root * root)
            scale[at(j, x, z), :] = root
            weight[at(j, x, z), :] = -base * root * root
            start[at(j, x, z), :] = diagonal * root
    for j in range(TURN):
        for x, z in TILES:
            here = scale[at(j, x, z), :]
            if x < SPAN_X - 1:
                cx[at_x(j, x, z), :] = cx[at_x(j, x, z), :] * here * scale[at(j, x + 1, z), :]
            after = scale[at(j + 1, x, z), :] if j < TURN - 1 else up_y(scale[at(0, x, z), :])
            cy[at(j, x, z), :] = cy[at(j, x, z), :] * here * after
            beside = up_z(scale[at(j, x, 0), :]) if z else scale[at(j, x, 1), :]
            cz[at(j, x, z), :] = cz[at(j, x, z), :] * here * beside
    for x, z in TILES:
        cw[at(0, x, z), :] = down_y(cy[at(TURN - 1, x, z), :])
    arrive(1)
    tiles = split([(initial, (x,)) for x in range(SPAN_X)], matrix)
    for j in range(TURN):
        for x, z in TILES:
            start[at(j, x, z), :] = start[at(j, x, z), :] * tiles(x, j, z)


def couple(cx, cy, cw, cz, begin, source, emit):
    def load(j):
        return {p: source[at(j, *p), :] for p in TILES}

    def wrap_down(row):
        return {p: cw[at(0, *p), :] * down_y(row[p]) for p in TILES}

    here = load(begin)
    before = load((begin - 1) % TURN)
    if begin == 0:
        before = wrap_down(before)
    else:
        before = {p: cy[at(begin - 1, *p), :] * before[p] for p in TILES}
    for turn in range(TURN):
        j = (begin + turn) % TURN
        following = load((j + 1) % TURN)
        after = following if j < TURN - 1 else {p: up_y(following[p]) for p in TILES}
        total, later = {}, {}
        for p in TILES:
            link = cy[at(j, *p), :]
            total[p] = before[p] + link * after[p]
            if j < TURN - 1:
                later[p] = link * here[p]
        for x in range(SPAN_X):
            even, odd = (x, 0), (x, 1)
            link = cz[at(j, *even), :]
            total[even] = total[even] + link * here[odd]
            total[odd] = total[odd] + link * here[even]
            link = cz[at(j, *odd), :]
            total[odd] = total[odd] + link * up_z(here[even])
            total[even] = total[even] + down_z(link * here[odd])
        for x in range(SPAN_X - 1):
            for z in range(2):
                link = cx[at_x(j, x, z), :]
                total[(x, z)] = total[(x, z)] + link * here[(x + 1, z)]
                total[(x + 1, z)] = total[(x + 1, z)] + link * here[(x, z)]
        emit(j, here, total)
        before = later if j < TURN - 1 else wrap_down(here)
        here = following


def kernel(first, final, *refs):
    refs = list(refs)
    take = lambda n: [refs.pop(0) for _ in range(n)]
    if first:
        far = take(8)
        outer_y, cx, cy, cw, cz, weight, scale, start, keep_x, keep_y, keep_z = take(11)
    else:
        (substeps,) = take(1)
        cx, cy, cw, cz, weight, scale, start, keep_x, keep_y, keep_z = take(10)
        face_low, face_high, come_y, come_z = take(4)
    if final:
        (field_out,) = take(1)
    out_low, out_high, out_y, out_z = take(4)
    if first:
        kcell, face_low, face_high, come_y, come_z = take(5)
        near = take(8)
        (arrivals,) = take(1)
    field, old, load, res, one, two, three = take(7)
    near_links, far_links = take(4), (cx, cy, cz, weight)
    if not first:
        for source, target in zip(far_links, near_links):
            target[...] = source[...]
    cx, cy, cz, weight = near_links
    lines, spare, turned_z, cols_z, sum_z = take(5)

    place_x, place_y, place_z = (lax.axis_index("gx"), lax.axis_index("gy"), lax.axis_index("gz"))
    planes_x = ((SPAN_X - 1) * place_z, (SPAN_X - 1) * (1 - place_z))
    outer_x = [jnp.where(plane == 0, 0, lax.axis_size("gx") - 1) for plane in planes_x]
    ends_x = [place_x == outer for outer in outer_x]
    lane, sub = lanes(), sublanes()

    if first:
        order = (2, 3, 4, 1, 0, 5, 6, 7)
        copies = {i: pltpu.make_async_copy(far[i], near[i], arrivals.at[i]) for i in order}
        for i in order:
            copies[i].start()
        initial, material, conduct, capacity, substeps, trace_x, trace_y, trace_z = near
        matrix = pairing(False)
        for i in (2, 3, 4, 1):
            copies[i].wait()
        steps = substeps[0]
        prepare(
            steps, matrix, lambda _: copies[0].wait(),
            initial, material, conduct, capacity, cx, cy, cw, cz, weight, scale, start, kcell,
        )
        for source, target in zip(near_links, far_links):
            target[...] = source[...]
        for i in (5, 6, 7):
            copies[i].wait()
        sides = (place_z, 1 - place_z)
        low_tiles, high_tiles = [split([(trace_x, (side, n)) for n in range(NT)], matrix) for side in sides]
        for n in range(NT):
            for j in range(TURN):
                for z in range(2):
                    tile = at_face(n, j, z)
                    face_low[tile, :] = low_tiles(n, j, z)
                    face_high[tile, :] = high_tiles(n, j, z)
                    keep_x[tile, :] = jnp.where(ends_x[0], low_tiles(n, j, z), high_tiles(n, j, z))
        for n in range(NT):
            for x in range(SPAN_X):
                keep_z[n, pl.ds(x, 1), :] = trace_z[n, place_z, pl.ds(x, 1), :]
                come_z[n, pl.ds(x, 1), :] = trace_z[n, 1 - place_z, pl.ds(x, 1), :]
                outer_y[n, pl.ds(x, 1), :] = trace_y[n, x, pl.ds(place_y, 1), :]
                for side in range(2):
                    spare[pl.ds(SUB * side + SPAN_X * n + x, 1), :] = trace_y[n, x, pl.ds(side, 1), :]
        both = spare[pl.ds(0, 2 * SUB), :]
        both = moved(jnp.concatenate([both, both], 1), matrix)
        for z in range(2):
            spare[pl.ds(2 * SUB * (z + 1), 2 * SUB), :] = both[:, z * SPAN : (z + 1) * SPAN]
        for n in range(NT):
            for i, (x, z) in enumerate(TILES):
                row = SPAN_X * n + x + 2 * SUB * (z + 1)
                keep_y[pl.ds(SUB * n + i, 1), :] = spare[pl.ds(row + SUB * place_y, 1), :]
                come_y[pl.ds(SUB * n + i, 1), :] = spare[pl.ds(row + SUB * (1 - place_y), 1), :]
    else:
        steps = substeps[0]
    last_part = jnp.where(steps == 2, F32(p_robin), F32(2.0 * p_robin))
    mid_part = jnp.where(steps == 2, F32(p_robin), F32(0.0))
    faces_x = ((planes_x[0], face_low, out_high), (planes_x[1], face_high, out_low))

    turned_z[...] = jnp.zeros((SPAN, SPAN), F32)
    inner_z = 1 - place_z
    for n in range(NT):
        for x in range(SPAN_X):
            row = 2 * (SPAN_X * n + x)
            for side, data in ((inner_z, come_z), (place_z, keep_z)):
                line = data[n, pl.ds(x, 1), :]
                place = row + (HALF - 1) * side
                turned_z[pl.ds(place, 1), :] = line
                turned_z[pl.ds((place + HALF) % SPAN, 1), :] = line
    cols_z[...] = turned_z[...].T
    outer_lanes = (lane < HALF // 2) | (lane >= SPAN - HALF // 2)
    low_half = outer_lanes == (lane % 2 == 0)
    for j in range(TURN):
        value = jnp.where(low_half, cols_z[rows_of(j, 0), :], cols_z[rows_of(j, 1), :])
        turned_z[pl.ds(SUB * j, SUB), :] = value
        sum_z[pl.ds(SUB * j, SUB), :] = jnp.zeros((SUB, SPAN), F32)
    for j in range(TURN):
        for p in TILES:
            value = start[at(j, *p), :]
            field[at(j, *p), :] = value
    end_even = (lane == 0) | (lane == HALF)
    end_odd = (lane == HALF - 1) | (lane == SPAN - 1)
    corner_low = (sub == 0) & (lane < HALF)
    corner_high = (sub == SUB - 1) & (lane >= HALF)

    if final:
        back = pairing(True)

    def coarse(n, nothing):
        tile_y = aligned(SUB * n)
        kept, come = keep_y[tile_y, :], come_y[tile_y, :]
        lines[pl.ds(0, SUB), :] = jnp.where(place_y == 0, kept, come)
        lines[pl.ds(SUB, SUB), :] = jnp.where(place_y == 0, come, kept)
        for j in range(TURN):
            column = turned_z[pl.ds(SUB * j, SUB), :]
            for x in range(SPAN_X):
                around = pltpu.roll(column, (SPAN - 2 * x - 2 * SPAN_X * n) % SPAN, 1)
                for z, ends in enumerate((end_even, end_odd)):
                    value = jnp.where(ends, around, 0.0)
                    line = 2 * x + z
                    if j == 0:
                        value = value + jnp.where(corner_low, lines[pl.ds(line, 1), :], 0.0)
                    if j == TURN - 1:
                        value = value + jnp.where(corner_high, lines[pl.ds(SUB + line, 1), :], 0.0)
                    load[at(j, x, z), :] = value * scale[at(j, x, z), :]
        for j in range(TURN):
            for z in range(2):
                tile = at_face(n, j, z)
                for end, (x, data, _) in zip(ends_x, faces_x):
                    value = jnp.where(end, keep_x[tile, :], data[tile, :])
                    at_x_face = aligned(at(j, 0, z).start + 2 * SUB * x)
                    load[at_x_face, :] = load[at_x_face, :] + value * scale[at_x_face, :]

        def substep(index, nothing):
            def to_res(j, here, total):
                for p in TILES:
                    tile = at(j, *p)
                    old[tile, :] = here[p]
                    res[tile, :] = total[p] + weight[tile, :] * here[p] + load[tile, :]

            def to_one(j, here, total):
                for p in TILES:
                    one[at(j, *p), :] = total[p] + here[p]

            def plain(out):
                def emit(j, here, total):
                    for p in TILES:
                        out[at(j, *p), :] = total[p]

                return emit

            def mixed(out, other, factor):
                def emit(j, here, total):
                    for p in TILES:
                        tile = at(j, *p)
                        out[tile, :] = total[p] + factor * other[tile, :]

                return emit

            def close(j, here, total):
                for p in TILES:
                    tile = at(j, *p)
                    field[tile, :] = old[tile, :] + GAIN * (total[p] + QUAD * res[tile, :])

            go = functools.partial(couple, cx, cy, cw, cz)
            go(0, field, to_res)
            go(1, res, to_one)
            go(2, one, plain(two))
            go(3, two, mixed(res, one, SHIFT))
            go(4, res, plain(one))
            go(5, one, mixed(two, res, -RHO2))
            go(6, two, plain(three))
            go(7, three, close)
            return nothing

        lax.fori_loop(0, steps, substep, 0)

        def mean(start_row, last, mid, step=1):
            if step == 1:
                rows = aligned(start_row)
            else:
                rows = pl.ds(start_row, SUB, stride=step)
            return scale[rows, :] * (last * field[rows, :] + mid * old[rows, :])

        planes = []
        for x, data, out in faces_x:
            made = []
            for j in range(TURN):
                pair = []
                for z in range(2):
                    tile = at_face(n, j, z)
                    pair.append(mean(at(j, 0, z).start + 2 * SUB * x, last_part, mid_part) - data[tile, :])
                    if not final:
                        out[tile, :] = pair[z]
                made.append(pair)
            planes.append((out, (n,), made))
        if final:
            join(planes, back)
        for j in range(TURN):
            gathered = sum_z[pl.ds(SUB * j, SUB), :]
            for x in range(SPAN_X):
                value = mean(at(j, x, 0).start + SUB * inner_z, last_part, mid_part)
                shift = 2 * x + 2 * SPAN_X * n
                mine = (lane - (HALF - 1) * inner_z - shift) % HALF == 0
                gathered = gathered + jnp.where(mine, pltpu.roll(value, shift, 1), 0.0)
            sum_z[pl.ds(SUB * j, SUB), :] = gathered
        corner = jnp.where(place_y == 0, at(TURN - 1, 0, 0).start + SUB - 1, 0)
        value = mean(corner, last_part, mid_part, SUB) - come_y[tile_y, :]
        if final:
            value = jnp.where((lane >= HALF) == (place_y == 0), value, other_half(value))
            spare[tile_y, :] = value
        else:
            out_y[tile_y, :] = other_half(value)
        return nothing

    for n in range(NT):
        coarse(n, 0)

    for j in range(TURN):
        value = sum_z[pl.ds(SUB * j, SUB), :]
        for half in range(2):
            turned_z[rows_of(j, half), :] = value
    cols_z[...] = turned_z[...].T
    line_lane = lax.broadcasted_iota(jnp.int32, (1, SPAN), 1)
    for n in range(NT):
        for x in range(SPAN_X):
            place = 2 * (SPAN_X * n + x) + (HALF - 1) * inner_z
            low, high = cols_z[pl.ds(place, 1), :], cols_z[pl.ds((place + HALF) % SPAN, 1), :]
            out_z[n, pl.ds(x, 1), :] = jnp.where(line_lane < HALF, low, high) - come_z[n, pl.ds(x, 1), :]
    if final:
        even, odd_z = spare[pl.ds(0, SUB, stride=2), :], spare[pl.ds(1, SUB, stride=2), :]
        both = jnp.concatenate([even, odd_z], 1)
        spare[pl.ds(2 * SUB, 2 * SUB), :] = moved(jnp.concatenate([both, both], 0), back)[:, :SPAN]
        for n in range(NT):
            for x in range(SPAN_X):
                out_y[n, pl.ds(x, 1), :] = spare[pl.ds(2 * SUB + SPAN_X * n + x, 1), :]
        field_out[...] = field[...] * scale[...]


def solve(first, final, *operands):
    vmem = pl.BlockSpec(memory_space=pltpu.VMEM)
    smem = pl.BlockSpec(memory_space=pltpu.SMEM)
    far = pl.BlockSpec(memory_space=pltpu.MemorySpace.HBM)
    wide = lambda rows: (rows, SPAN)
    lines_z = (NT, SPAN_X, SPAN)
    if first:
        in_specs = [far] * 8
    else:
        in_specs = [smem] + [vmem] * 14
    shapes = []
    if first:
        shapes += [lines_z, wide(ROWS_X), wide(ROWS), wide(len(TILES) * SUB)] + [wide(ROWS)] * 4
        shapes += [wide(NT * ROWS_A), wide(NT * SUB), lines_z]
    if final:
        shapes += [wide(ROWS)]
    shapes += [(NT, SPAN, SPAN) if final else wide(NT * ROWS_A)] * 2
    shapes += [lines_z if final else wide(NT * SUB), lines_z]
    scratch = []
    if first:
        scratch += [pltpu.VMEM(wide(ROWS), F32)] + [pltpu.VMEM(wide(NT * ROWS_A), F32)] * 2
        scratch += [pltpu.VMEM(wide(NT * SUB), F32), pltpu.VMEM(lines_z, F32)]
        for i, operand in enumerate(operands):
            space = pltpu.SMEM if i in (2, 3, 4) else pltpu.VMEM
            scratch.append(space(operand.shape, operand.dtype))
        scratch.append(pltpu.SemaphoreType.DMA((8,)))
    scratch += [pltpu.VMEM(wide(ROWS), F32)] * 7
    scratch += [pltpu.VMEM(wide(ROWS_X), F32)] + [pltpu.VMEM(wide(ROWS), F32)] * 3
    scratch += [pltpu.VMEM(wide(2 * SUB), F32), pltpu.VMEM(wide(6 * SUB), F32)]
    scratch += [pltpu.VMEM(wide(SPAN), F32)] * 2 + [pltpu.VMEM(wide(TURN * SUB), F32)]
    return pl.pallas_call(
        functools.partial(kernel, first, final),
        out_shape=[jax.ShapeDtypeStruct(shape, F32) for shape in shapes],
        in_specs=in_specs,
        out_specs=[vmem] * len(shapes),
        scratch_shapes=scratch,
        compiler_params=pltpu.CompilerParams(vmem_limit_bytes=24 * 1024 * 1024),
    )(*operands)


def unfold(field, out):
    planes = []
    for x in range(SPAN_X):
        made = [[field[at(j, x, z), :] for z in range(2)] for j in range(TURN)]
        planes.append((out, (x,), made))
    join(planes, pairing(True))


def exchange(out_low, out_high, out_y, out_z):
    count = lax.axis_size("gx")
    cores = lax.axis_size("gz")

    def turn(way):
        pairs = []
        for i in range(count):
            for z in range(cores):
                to = i + (way if z == 0 else -way)
                pairs.append((i * cores + z, to * cores + z if 0 <= to < count else i * cores + 1 - z))
        return pairs

    swap = [(0, 1), (1, 0)]
    return (
        lax.ppermute(out_low, ("gx", "gz"), turn(1)),
        lax.ppermute(out_high, ("gx", "gz"), turn(-1)),
        lax.ppermute(out_y, "gy", swap),
        lax.ppermute(out_z, "gz", swap),
    )


def local(initial, material, conduct, capacity, substeps, trace_x, trace_y, trace_z):
    steps = substeps.reshape(1)
    place_x, place_y, place_z = (lax.axis_index("gx"), lax.axis_index("gy"), lax.axis_index("gz"))
    inputs = (initial, material, conduct, capacity, steps, trace_x, trace_y, trace_z)
    hold = lambda value: pltpu.with_memory_space_constraint(value, pltpu.MemorySpace.HBM)
    inputs = [value if value is steps else hold(value) for value in inputs]
    results = solve(True, False, *inputs)
    outer_y, *prepared = results[:11]
    outer_z, sent = prepared[-1], results[11:]
    for iteration in range(1, ITERS):
        arrived = exchange(*sent)
        final = iteration == ITERS - 1
        sent = solve(False, final, steps, *prepared, *arrived)
    field, *sent = sent
    face_low, face_high, come_y, come_z = exchange(*sent)
    face_low, face_high = (
        jnp.where(place_z == 0, face_low, face_high),
        jnp.where(place_z == 0, face_high, face_low),
    )
    face_low = jnp.where(place_x == 0, trace_x[0], face_low)
    face_high = jnp.where(place_x == lax.axis_size("gx") - 1, trace_x[1], face_high)
    got_x = jnp.stack([face_low, face_high], 0)
    got_y = jnp.stack([jnp.where(place_y == side, outer_y, come_y) for side in range(2)], 2)
    got_z = jnp.stack([jnp.where(place_z == side, outer_z, come_z) for side in range(2)], 1)
    vmem = pl.BlockSpec(memory_space=pltpu.VMEM)
    thermal = pl.pallas_call(
        unfold,
        out_shape=jax.ShapeDtypeStruct((SPAN_X, SPAN, SPAN), F32),
        in_specs=[vmem],
        out_specs=vmem,
        cost_estimate=pl.CostEstimate(flops=10**8, bytes_accessed=10**6, transcendentals=0),
    )(pltpu.with_memory_space_constraint(field, pltpu.MemorySpace.VMEM))
    return (thermal, got_x, got_y, got_z)


def solution(mesh):
    placed = (
        P("gx", "gy", "gz"),
        P("gx", "gy", "gz"),
        P(),
        P(),
        P("gx", "gy", "gz"),
        P("gx", None, "gy", "gz"),
        P(None, "gx", "gy", "gz"),
        P(None, "gz", "gx", "gy"),
    )
    return jax.shard_map(
        local,
        mesh=mesh,
        in_specs=placed,
        out_specs=(
            P("gx", "gy", "gz"),
            P("gx", None, "gy", "gz"),
            P(None, "gx", "gy", "gz"),
            P(None, "gz", "gx", "gy"),
        ),
        check_vma=False,
    )
```
